32 devices in a mesh: gx: 8 (over y, x, core), gy: 4 (over z).
Axes of the slice: x: 2, y: 2, z: 4, core: 2. Of those that a mesh axis runs over, the one named last changes fastest.
Arguments:
- cotangent: float32 [3, 16, 8, 128], P(None, 'gx', 'gy'), may hold values from -4 to 4
- polarizability: float32 [16, 8, 128], P('gx', 'gy'), may hold values from 0.2 to 1.6
- site_offset: int32 [3, 16, 8, 128], P(None, 'gx', 'gy'), may hold values from 0 to 15, as said below
- site_fraction: float32 [3, 16, 8, 128], P(None, 'gx', 'gy'), may hold values from 0.2 to 0.8
- cell_count: int32 [16, 8, 16], P('gx', 'gy'), may hold values from 4 to 8, as said below
Outputs:
- adjoint_dipoles: float32 [3, 16, 8, 128], P(None, 'gx', 'gy')
The draws below stay inside these ranges and needn't reach their ends.
Inputs may be any that keep to these rules, and one draw needn't show every extreme that they name: `site_offset`: within a cell the 8 slots name distinct mesh points: no two slots have the same three components. The first component is below 8, the second below 8, the third below 16. `cell_count`: some cell holds 8 live atoms.
All inputs are finite; a program needn't handle non-finite values.
Results may differ from the reference program's by a relative error of at most 0.0001.
Values sent between devices are 32-bit elements; how exact they have to be, the bound alone decides.
No kernel may reach another device: no remote copies, remote signals or barrier semaphores. Data moves between devices by JAX's collectives and lax.ppermute only.
A program may use at most 128 MiB of HBM per device.

```python
import math
import jax
import jax.numpy as jnp
from jax import lax

A = 8
NCZ = 16
HX = 8
HY = 8
HZ = 16
ITERS = 2
NCX = 16
NCY = 8
KX = 128
KY = 64
KZ = 256


def draw_cotangent(key, part):
    shape = (3, NCX, NCY, NCZ * A)
    return jnp.clip(jax.random.normal(jax.random.fold_in(key, 43), shape, jnp.float32), -4.0, 4.0)


def draw_site_offset(key, part):
    count = NCX * NCY * NCZ
    keys = jax.random.split(jax.random.fold_in(key, 11), count)

    def pick(one_key):
        return jax.random.permutation(one_key, HX * HY * HZ)[:A]
    chosen = jax.vmap(pick)(keys).astype(jnp.int32).reshape(NCX, NCY, NCZ * A)
    first = chosen // (HY * HZ)
    second = chosen // HZ % HY
    third = chosen % HZ
    return jnp.stack([first, second, third], axis=0)


def draw_cell_count(key, part):
    count = NCX * NCY * NCZ
    base = jax.random.randint(jax.random.fold_in(key, 23), (NCX, NCY, NCZ), A // 2, A + 1, dtype=jnp.int32)
    chosen = jax.random.randint(jax.random.fold_in(key, 29), (), 0, count, dtype=jnp.int32)
    flat = jnp.arange(count, dtype=jnp.int32).reshape(NCX, NCY, NCZ)
    return jnp.where(flat == chosen, A, base).astype(jnp.int32)


def levels(key, extent, cuts, least, high):
    gain = 1.0
    for position, shards_of in cuts:
        heights = jax.random.uniform(jax.random.fold_in(jax.random.fold_in(key, 6), position), (shards_of,), jnp.float32, least / len(cuts), high / len(cuts))
        gain = gain * jnp.repeat(jnp.exp(heights), extent[position] // shards_of).reshape((-1,) + (1,) * (len(extent) - 1 - position))
    return gain


def setup_inputs(seed: int = 0) -> dict:
    key_of = jax.random.split(jax.random.key(seed), 6)
    return {
        "cotangent": draw_cotangent(jax.random.fold_in(key_of[5], 71), 0),
        "polarizability": jnp.clip(jnp.exp(math.log(1.6) - 2.0794415 * jax.random.uniform(key_of[1], (NCX, NCY, NCZ * A), jnp.float32) ** levels(key_of[1], (NCX, NCY, NCZ * A), ((0, 8), (1, 4)), -0.2, 0.2)), 0.2, 1.6),
        "site_offset": draw_site_offset(jax.random.fold_in(key_of[5], 71), 0),
        "site_fraction": jnp.clip(0.2 + 0.6 * jax.random.uniform(key_of[3], (3, NCX, NCY, NCZ * A), jnp.float32) ** levels(key_of[3], (3, NCX, NCY, NCZ * A), ((1, 8), (2, 4)), -0.2, 0.2), 0.2, 0.8),
        "cell_count": draw_cell_count(jax.random.fold_in(key_of[5], 71), 0),
    }


BETA = 0.7
THOLE = 0.39
ROOT_PI = 1.7724538509055159
SELF_GAIN = 4.0 * BETA * BETA * BETA / (3.0 * ROOT_PI)
NEIGHBOUR_SHIFTS = [(a, b, c) for a in (-1, 0, 1) for b in (-1, 0, 1) for c in (-1, 0, 1)]

def coefficients(square, root):
    distance = jnp.sqrt(square)
    inverse_square = 1.0 / square
    screened = jax.scipy.special.erfc(BETA * distance) / distance
    gauss = 2.0 * BETA / ROOT_PI * jnp.exp(-BETA * BETA * square)
    first = (screened + gauss) * inverse_square
    second = (3.0 * first + 2.0 * BETA * BETA * gauss) * inverse_square
    scaled = THOLE * square * distance / root
    damping = jnp.exp(-scaled)
    inverse_cube = inverse_square / distance
    first = first - damping * inverse_cube
    second = second - 3.0 * (1.0 + scaled) * damping * inverse_cube * inverse_square
    return (first, second)

def pair_terms(place_own, polar_own, place_near, polar_near, self_pair):
    separation = place_own[:, :, :, None] - place_near[:, :, None, :]
    square = separation[0] * separation[0] + separation[1] * separation[1] + separation[2] * separation[2]
    square = jnp.where(self_pair, 1.0, square)
    root = jnp.sqrt(polar_own[:, :, None] * polar_near[:, None, :])
    first, second = coefficients(square, root)
    first = jnp.where(self_pair, 0.0, first)
    second = jnp.where(self_pair, 0.0, second)
    return (separation, first, second)

def pair_apply(separation, first, second, moment_near):
    along = moment_near[:, :, None, :]
    projected = lax.optimization_barrier(jnp.sum(separation * along, axis=0))
    return lax.optimization_barrier(jnp.sum(second * projected * separation - first * along, axis=3))

def spline(fraction):
    rest = 1.0 - fraction
    square = fraction * fraction
    cube = square * fraction
    values = jnp.stack([rest * rest * rest / 6.0, (3.0 * cube - 6.0 * square + 4.0) / 6.0, (-3.0 * cube + 3.0 * square + 3.0 * fraction + 1.0) / 6.0, cube / 6.0], axis=-1)
    slopes = jnp.stack([-0.5 * rest * rest, 0.5 * (3.0 * square - 4.0 * fraction), 0.5 * (-3.0 * square + 2.0 * fraction + 1.0), 0.5 * square], axis=-1)
    return (values, slopes)

def neighbour_stack(cells):
    pieces = []
    for across, along, upward in NEIGHBOUR_SHIFTS:
        pieces.append(jnp.roll(cells, (-across, -along, -upward), axis=(1, 2, 3)))
    return jnp.stack(pieces, axis=4)

def by_column(values):
    return jnp.transpose(values, (1, 0, 2, 3, 4)).reshape(NCX, values.shape[0], NCY * NCZ, values.shape[4])

def green_table(dtype):

    def part(length):
        grid = jnp.arange(length, dtype=jnp.int32)
        signed = jnp.where(2 * grid < length, grid, grid - length).astype(dtype) / length
        angle = 2.0 * math.pi / length * grid.astype(dtype)
        factor = 9.0 / ((2.0 + jnp.cos(angle)) * (2.0 + jnp.cos(angle)))
        return (grid, signed * signed, factor)
    grid_x, square_x, factor_x = part(KX)
    grid_y, square_y, factor_y = part(KY)
    grid_z, square_z, factor_z = part(KZ)
    square = square_x[:, None, None] + square_y[None, :, None] + square_z[None, None, :]
    anchor = (grid_x[:, None, None] == 0) & (grid_y[None, :, None] == 0) & (grid_z[None, None, :] == 0)
    safe = jnp.where(anchor, 1.0, square)
    value = jnp.exp(-(math.pi / BETA) * (math.pi / BETA) * safe) / (math.pi * safe)
    value = value * factor_x[:, None, None] * factor_y[None, :, None] * factor_z[None, None, :]
    return jnp.where(anchor, 0.0, value)

def reference(cotangent, polarizability, site_offset, site_fraction, cell_count):
    dtype = cotangent.dtype
    slot = jnp.arange(A, dtype=jnp.int32)
    live = (slot < cell_count[..., None]).astype(dtype).reshape(NCX, NCY, NCZ * A)
    place = site_offset.astype(dtype) + 1.0 + site_fraction
    shifts = jnp.asarray(NEIGHBOUR_SHIFTS, dtype=dtype).T * jnp.asarray([HX, HY, HZ], dtype=dtype)[:, None]
    place_cells = place.reshape(3, NCX, NCY, NCZ, A)
    polar_cells = polarizability.reshape(1, NCX, NCY, NCZ, A)
    moved = neighbour_stack(place_cells) + shifts[:, None, None, None, :, None]
    place_near = by_column(moved.reshape(3, NCX, NCY, NCZ, 27 * A))
    polar_near = by_column(neighbour_stack(polar_cells).reshape(1, NCX, NCY, NCZ, 27 * A))[:, 0]
    place_own = by_column(place_cells)
    polar_own = by_column(polar_cells)[:, 0]
    index = jnp.arange(27 * A, dtype=jnp.int32)
    self_pair = (index[None, :] // A == 13) & (index[None, :] % A == slot[:, None])

    def column_field(item):
        separation, first, second = pair_terms(item[0], item[1], item[2], item[3], self_pair)
        return pair_apply(separation, first, second, item[4])

    def near_field(moment):
        cells = moment.reshape(3, NCX, NCY, NCZ, A)
        moment_near = by_column(neighbour_stack(cells).reshape(3, NCX, NCY, NCZ, 27 * A))
        blocks = lax.map(column_field, (place_own, polar_own, place_near, polar_near, moment_near))
        return jnp.transpose(blocks, (1, 0, 2, 3)).reshape(3, NCX, NCY, NCZ * A)
    cell_x = jnp.arange(NCX, dtype=jnp.int32)[:, None, None]
    cell_y = jnp.arange(NCY, dtype=jnp.int32)[None, :, None]
    cell_z = (jnp.arange(NCZ * A, dtype=jnp.int32) // A)[None, None, :]
    corner = jnp.arange(4, dtype=jnp.int32)
    grid_x = ((cell_x * HX + site_offset[0]).reshape(-1)[:, None] + corner) % KX
    grid_y = ((cell_y * HY + site_offset[1]).reshape(-1)[:, None] + corner) % KY
    grid_z = ((cell_z * HZ + site_offset[2]).reshape(-1)[:, None] + corner) % KZ
    values_x, slopes_x = spline(site_fraction[0].reshape(-1))
    values_y, slopes_y = spline(site_fraction[1].reshape(-1))
    values_z, slopes_z = spline(site_fraction[2].reshape(-1))
    gather_index = (grid_x[:, :, None, None], grid_y[:, None, :, None], grid_z[:, None, None, :])
    slope_first = slopes_x[:, :, None, None] * values_y[:, None, :, None] * values_z[:, None, None, :]
    slope_second = values_x[:, :, None, None] * slopes_y[:, None, :, None] * values_z[:, None, None, :]
    slope_third = values_x[:, :, None, None] * values_y[:, None, :, None] * slopes_z[:, None, None, :]
    green = green_table(dtype)

    def far_field(moment):
        flat = moment.reshape(3, -1)
        weight = flat[0][:, None, None, None] * slope_first + flat[1][:, None, None, None] * slope_second + flat[2][:, None, None, None] * slope_third
        charge = jnp.zeros((KX, KY, KZ), dtype).at[gather_index].add(weight)
        potential = jnp.real(jnp.fft.ifftn(green * jnp.fft.fftn(charge))).astype(dtype)
        sampled = potential[gather_index]
        field = jnp.stack([-lax.optimization_barrier(jnp.sum(slope_first * sampled, axis=(1, 2, 3))), -lax.optimization_barrier(jnp.sum(slope_second * sampled, axis=(1, 2, 3))), -lax.optimization_barrier(jnp.sum(slope_third * sampled, axis=(1, 2, 3)))], axis=0)
        return field.reshape(3, NCX, NCY, NCZ * A)
    moment = live * polarizability * cotangent
    for turn in range(ITERS):
        field = near_field(moment) + far_field(moment) + SELF_GAIN * moment
        moment = live * polarizability * (cotangent + field)
    return moment
```

```python
import functools
import math

import jax
import jax.numpy as jnp
import ml_dtypes
import numpy as np
from jax import lax
from jax.experimental import pallas as pl
from jax.experimental.pallas import tpu as pltpu
from jax.sharding import PartitionSpec as P

A = 8
HX = 8
HY = 8
HZ = 16
ITERS = 2
BETA = 0.7
THOLE = 0.39
ROOT_PI = 1.7724538509055159
SELF_GAIN = 4.0 * BETA * BETA * BETA / (3.0 * ROOT_PI)
MODES = 8
SPAN = 16
AXES = ("gx", "gy")
F32 = jnp.float32
BF16 = jnp.bfloat16
VMEM_LIMIT = 56 * 1024 * 1024


def two_terms(table):
    high = table.astype(ml_dtypes.bfloat16)
    low = (table - high.astype(np.float64)).astype(ml_dtypes.bfloat16)
    return high, low


def cas_table(length):
    grid = np.arange(length, dtype=np.int64)
    angle = 2.0 * np.pi / length * (grid[:, None] * grid[None, :] % length)
    return np.cos(angle) + np.sin(angle)


def x_tables(cells, length):
    cas = cas_table(length)
    place = (np.arange(cells)[:, None] * HX + np.arange(SPAN)[None, :]) % length
    forward = np.broadcast_to(cas[place][:, None], (cells, 2, SPAN, length))
    forward = forward.reshape(cells // 4, 4 * 2 * SPAN, length)
    inverse = np.broadcast_to(cas[place][:, None], (cells, 4, SPAN, length))
    inverse = inverse.reshape(cells // 2, 2 * 4 * SPAN, length).transpose(0, 2, 1)
    return two_terms(forward), two_terms(inverse)


def split(value):
    high = value.astype(BF16)
    low = (value - high.astype(F32)).astype(BF16)
    return high, low


def dot(left, right):
    return jnp.dot(left, right, preferred_element_type=F32)


def dot_nt(left, right):
    return lax.dot_general(left, right, (((1,), (1,)), ((), ())), preferred_element_type=F32)


def spline(fraction):
    rest = 1.0 - fraction
    square = fraction * fraction
    cube = square * fraction
    values = (
        rest * rest * rest / 6.0,
        (3.0 * cube - 6.0 * square + 4.0) / 6.0,
        (-3.0 * cube + 3.0 * square + 3.0 * fraction + 1.0) / 6.0,
        cube / 6.0,
    )
    slopes = (
        -0.5 * rest * rest,
        0.5 * (3.0 * square - 4.0 * fraction),
        0.5 * (-3.0 * square + 2.0 * fraction + 1.0),
        0.5 * square,
    )
    return values, slopes


def basis(anchor, weights):
    lanes = anchor.shape[1]
    index = lax.broadcasted_iota(jnp.int32, (SPAN, lanes), 0) - anchor
    total = jnp.zeros((SPAN, lanes), F32)
    for order in range(4):
        total = jnp.where(index == order, weights[order], total)
    return total


def turns(count, length):
    part = count.astype(F32) * (1.0 / length)
    half = math.pi * jnp.where(2 * count >= length, part - 1.0, part)
    square = half * half
    sine = 1.0
    for order in (10, 8, 6, 4, 2):
        sine = 1.0 - square * sine * (1.0 / (order * (order + 1)))
    sine = sine * half
    cosine = 1.0
    for order in (11, 9, 7, 5, 3, 1):
        cosine = 1.0 - square * cosine * (1.0 / (order * (order + 1)))
    return 1.0 - 2.0 * sine * sine, 2.0 * sine * cosine


def pack_kernel(cot_ref, polar_ref, offset_ref, fraction_ref, count_ref, send_ref, gain_ref):
    cells_x, cells_y, lanes = polar_ref.shape
    devices = send_ref.shape[0]
    cells = lanes // A
    row = lax.broadcasted_iota(jnp.int32, (cells, lanes), 0)
    lane = lax.broadcasted_iota(jnp.int32, (cells, lanes), 1)
    widen = jnp.where(lane // A == row, 1.0, 0.0)
    slot = (lax.broadcasted_iota(jnp.int32, (cells_y, lanes), 1) % A).astype(F32)
    rows = [[] for _ in range(7)]
    gains = []
    for cx in range(cells_x):
        count = dot(count_ref[cx].astype(F32), widen)
        gain = jnp.where(slot < count, polar_ref[cx], 0.0)
        gains.append(gain)
        for axis in range(3):
            place = offset_ref[axis, cx].astype(F32) + 1.0 + fraction_ref[axis, cx]
            rows[axis].append(place)
            rows[3 + axis].append(gain * cot_ref[axis, cx])
        rows[6].append(polar_ref[cx])
    gain_ref[...] = jnp.concatenate(gains, axis=0)
    block = jnp.stack([jnp.concatenate(parts, axis=0) for parts in rows], axis=0)

    def put(d, carry):
        send_ref[d] = block
        return carry

    lax.fori_loop(0, devices, put, 0)


def far_kernel(
    shape,
    place_ref,
    moment_ref,
    mode_ref,
    phase_ref,
    green_ref,
    fx_high_ref,
    fx_low_ref,
    ix_high_ref,
    ix_low_ref,
    y_ref,
    out_ref,
    cell_ref,
    line_ref,
    back_ref,
    wave_ref,
    side_ref,
    rise_ref,
    edge_ref,
):
    devices_x, devices_y, cells_x, cells_y, points_z = shape
    columns = cells_x * cells_y
    lanes = place_ref.shape[3]
    length_x = green_ref.shape[1]
    length_y = y_ref.shape[0]
    tall = length_y * MODES
    spill = 3 * MODES
    reach = (HY + 3) * MODES
    per_cell = HY * MODES
    turn_x = 4 // cells_x
    keep = side_ref.shape[0] > 1
    layer = (lax.broadcasted_iota(jnp.int32, (1, lanes), 1) // A) * HZ
    cell_ref[...] = jnp.zeros_like(cell_ref)

    def statics(d, l):
        k = d if keep else 0
        place = [place_ref[d, axis, l : l + 1, :] for axis in range(3)]
        whole = [jnp.floor(value) for value in place]
        parts = [spline(value - low) for value, low in zip(place, whole)]
        anchor = [low.astype(jnp.int32) - 1 for low in whole]
        values_x = basis(anchor[0], parts[0][0])
        slopes_x = basis(anchor[0], parts[0][1])
        side = jnp.concatenate([slopes_x, values_x], axis=1)
        high, low = split(side)
        side_ref[k, l] = jnp.concatenate([high, low], axis=0)
        rise_ref[k, l] = jnp.concatenate(
            [basis(anchor[1], parts[1][0]), basis(anchor[1], parts[1][1])], axis=0
        )
        phase = lax.rem(mode_ref[...] * (anchor[2] + layer), points_z)
        cosine, sine = turns(phase, points_z)
        found = []
        for weights in parts[2]:
            plus = weights[0] * phase_ref[0]
            minus = weights[0] * phase_ref[4]
            for order in range(1, 4):
                plus = plus + weights[order] * phase_ref[order]
                minus = minus + weights[order] * phase_ref[4 + order]
            found.append(cosine * plus + sine * minus)
        edge_ref[k, l] = jnp.concatenate(found, axis=0)

    def spread(d, l, slot, group, start):
        k = d if keep else 0
        first = edge_ref[k, l, :MODES] * moment_ref[d, 0, l : l + 1, :]
        second = edge_ref[k, l, :MODES] * moment_ref[d, 1, l : l + 1, :]
        third = edge_ref[k, l, MODES:] * moment_ref[d, 2, l : l + 1, :]
        tiles = []
        for y in range(HY + 3):
            value = rise_ref[k, l, y : y + 1, :]
            slope = rise_ref[k, l, SPAN + y : SPAN + y + 1, :]
            tile = jnp.concatenate([value * first, slope * second + value * third], axis=1)
            rest = tile - tile.astype(BF16).astype(F32)
            tiles.append(jnp.concatenate([tile, rest], axis=0).astype(BF16))
        sums = jnp.concatenate(tiles, axis=0)
        pieces = []
        if slot:
            pieces.append(jnp.zeros((slot * 2 * SPAN, 2 * lanes), BF16))
        pieces.append(side_ref[k, l])
        if slot < 3:
            pieces.append(jnp.zeros(((3 - slot) * 2 * SPAN, 2 * lanes), BF16))
        got = dot_nt(sums, jnp.concatenate(pieces, axis=0))
        got = got.reshape(HY + 3, 2, MODES, got.shape[1])
        got = (got[:, 0] + got[:, 1]).reshape(reach, got.shape[3])
        cell_ref[group, pl.ds(start, reach), :] = cell_ref[group, pl.ds(start, reach), :] + got

    def spread_row(pair, carry):
        for odd in range(turn_x):
            gx = pair * turn_x + odd

            def spread_device(gy, inner):
                d = gx * devices_y + gy
                for l in range(columns):
                    statics(d, l)
                for l in range(columns):
                    slot = odd * cells_x + l // cells_y
                    start = pl.multiple_of(
                        (gy * cells_y + l % cells_y) * per_cell, per_cell
                    )
                    spread(d, l, slot, pair, start)
                return inner

            lax.fori_loop(0, devices_y, spread_device, 0)
        return carry

    lax.fori_loop(0, devices_x // turn_x, spread_row, 0)

    cell_ref[:, :spill, :] = cell_ref[:, :spill, :] + cell_ref[:, tall : tall + spill, :]
    total = jnp.zeros((tall, length_x), F32)
    for group in range(cell_ref.shape[0]):
        high, low = split(cell_ref[group, :tall, :])
        total = total + (
            dot(high, fx_high_ref[group])
            + dot(low, fx_high_ref[group])
            + dot(high, fx_low_ref[group])
        )
    blocks = length_x // line_ref.shape[2]
    width = line_ref.shape[2]
    for block in range(blocks):
        line_ref[block] = total[:, block * width : (block + 1) * width]

    def along_y(value):
        high, low = split(value)
        return dot(y_ref[...], jnp.concatenate([high, high, low], axis=0))

    for mode in range(MODES):
        for block in range(blocks):
            got = along_y(line_ref[block, pl.ds(mode, length_y, stride=MODES), :])
            got = got * green_ref[
                mode * length_y : (mode + 1) * length_y, block * width : (block + 1) * width
            ]
            back_ref[block, pl.ds(mode, length_y, stride=MODES), :] = along_y(got)
    high, low = split(jnp.concatenate([back_ref[block] for block in range(blocks)], axis=1))
    lane = lax.broadcasted_iota(jnp.int32, (tall, 2 * 4 * SPAN), 1)
    rest = lane // SPAN % 2 == 1
    for group in range(wave_ref.shape[0]):
        got = (
            dot(high, ix_high_ref[group])
            + dot(low, ix_high_ref[group])
            + dot(high, ix_low_ref[group])
        )
        got = jnp.where(rest, got - got.astype(BF16).astype(F32), got).astype(BF16)
        wave_ref[group, :tall, :] = got
        wave_ref[group, tall:, :] = got[: wave_ref.shape[1] - tall]

    window = -(-reach // 16) * 16

    def gather(d, l, slot, group, start):
        k = d if keep else 0
        high = side_ref[k, l, :SPAN]
        low = side_ref[k, l, SPAN:]
        block = [high, high, low, low]
        zero = jnp.zeros((4 * SPAN, 2 * lanes), BF16)
        pieces = [zero] + block if slot else block + [zero]
        got = dot(wave_ref[group, pl.ds(start, window), :], jnp.concatenate(pieces, axis=0))
        sums = [jnp.zeros((MODES, lanes), F32) for _ in range(3)]
        for y in range(HY + 3):
            value = rise_ref[k, l, y : y + 1, :]
            slope = rise_ref[k, l, SPAN + y : SPAN + y + 1, :]
            sloped = got[y * MODES : (y + 1) * MODES, :lanes]
            plain = got[y * MODES : (y + 1) * MODES, lanes:]
            sums[0] = sums[0] + sloped * value
            sums[1] = sums[1] + plain * slope
            sums[2] = sums[2] + plain * value
        value = edge_ref[k, l, :MODES]
        slope = edge_ref[k, l, MODES:]
        for axis, part in enumerate((value, value, slope)):
            out_ref[d, axis, l : l + 1, :] = -jnp.sum(sums[axis] * part, axis=0, keepdims=True)

    def gather_row(gx, carry):
        def gather_device(gy, inner):
            d = gx * devices_y + gy
            if not keep:
                for l in range(columns):
                    statics(d, l)
            for l in range(columns):
                across = l // cells_y
                start = pl.multiple_of((gy * cells_y + l % cells_y) * per_cell, per_cell)
                group = (gx * cells_x + across - across % 2) // 2
                gather(d, l, across % 2, group, start)
            return inner

        lax.fori_loop(0, devices_y, gather_device, 0)
        return carry

    lax.fori_loop(0, devices_x, gather_row, 0)


def near_kernel(shape, where_ref, static_ref, moment_ref, out_ref, raw_ref, wide_ref, sum_ref):
    devices_x, devices_y, cells_x, cells_y = shape
    lanes = static_ref.shape[3]
    rows_x, rows_y = cells_x + 2, cells_y + 2
    total_x, total_y = devices_x * cells_x, devices_y * cells_y
    lane = lax.broadcasted_iota(jnp.int32, (A, lanes), 1)
    sub = lax.broadcasted_iota(jnp.int32, (A, lanes), 0)
    own = lane % A == sub
    for a in range(rows_x):
        for b in range(rows_y):
            cell_x = lax.rem(where_ref[0] * cells_x + (a - 1 + total_x), total_x)
            cell_y = lax.rem(where_ref[1] * cells_y + (b - 1 + total_y), total_y)
            d = (cell_x // cells_x) * devices_y + cell_y // cells_y
            l = lax.rem(cell_x, cells_x) * cells_y + lax.rem(cell_y, cells_y)
            for item in range(7):
                if item < 4:
                    row = static_ref[d, item if item < 3 else 6, pl.ds(l, 1), :]
                else:
                    row = moment_ref[d, item - 4, pl.ds(l, 1), :]
                first = ((a * rows_y + b) * 7 + item) * A
                raw_ref[first : first + A, :] = jnp.where(own, row, 0.0)
    group = lax.broadcasted_iota(jnp.int32, (lanes, lanes), 0) // A
    other = lax.broadcasted_iota(jnp.int32, (lanes, lanes), 1) // A
    ones = jnp.where(group == other, 1.0, 0.0).astype(BF16)
    raw = raw_ref[...]
    high = raw.astype(BF16)
    raw = raw - high.astype(F32)
    middle = raw.astype(BF16)
    low = (raw - middle.astype(F32)).astype(BF16)
    wide = dot(low, ones) + dot(middle, ones) + dot(high, ones)
    wide_ref[...] = wide.reshape(wide_ref.shape)

    for across in range(cells_x):
        for along in range(cells_y):
            mine = (across + 1) * rows_y + along + 1
            mine_d = where_ref[0] * devices_y + where_ref[1]
            mine_l = across * cells_y + along
            at = [static_ref[mine_d, axis, mine_l : mine_l + 1, :] for axis in range(3)]
            polar = static_ref[mine_d, 6, mine_l : mine_l + 1, :]
            sum_ref[...] = jnp.zeros_like(sum_ref)

            def visit(step, carry, across=across, along=along, at=at, polar=polar):
                dx = step // 3 - 1
                dy = lax.rem(step, 3) - 1
                found = (across + 1 + dx) * rows_y + along + 1 + dy
                shift_x = dx.astype(F32) * HX
                shift_y = dy.astype(F32) * HY
                sums = [sum_ref[axis] for axis in range(3)]
                for dz in (-1, 0, 1):
                    near = [wide_ref[found, item] for item in range(7)]
                    if dz:
                        near = [pltpu.roll(v, (-dz * A) % lanes, 1) for v in near]
                    r0 = at[0] - near[0] - shift_x
                    r1 = at[1] - near[1] - shift_y
                    r2 = at[2] - near[2] - float(dz * HZ)
                    square = r0 * r0 + r1 * r1 + r2 * r2
                    if dz == 0:
                        selfish = own & (step == 4)
                        square = jnp.where(selfish, 1.0, square)
                    inverse = lax.rsqrt(square)
                    inverse_square = inverse * inverse
                    distance = square * inverse
                    root_inverse = lax.rsqrt(polar * near[3])
                    t = 1.0 / (1.0 + (0.5 * BETA) * distance)
                    series = 0.17087277
                    for c in (-0.82215223, 1.48851587, -1.13520398, 0.27886807,
                              -0.18628806, 0.09678418, 0.37409196, 1.00002368, -1.26551223):
                        series = series * t + c
                    bell = jnp.exp((-BETA * BETA) * square)
                    screened = t * jnp.exp(series) * bell * inverse
                    gauss = (2.0 * BETA / ROOT_PI) * bell
                    first = (screened + gauss) * inverse_square
                    second = (3.0 * first + (2.0 * BETA * BETA) * gauss) * inverse_square
                    scaled = THOLE * square * distance * root_inverse
                    damping = jnp.exp(-scaled) * (inverse_square * inverse)
                    first = first - damping
                    second = second - 3.0 * (1.0 + scaled) * damping * inverse_square
                    if dz == 0:
                        first = jnp.where(selfish, 0.0, first)
                        second = jnp.where(selfish, 0.0, second)
                    projected = second * (r0 * near[4] + r1 * near[5] + r2 * near[6])
                    sums[0] = sums[0] + (projected * r0 - first * near[4])
                    sums[1] = sums[1] + (projected * r1 - first * near[5])
                    sums[2] = sums[2] + (projected * r2 - first * near[6])
                for axis in range(3):
                    sum_ref[axis] = sums[axis]
                return carry

            lax.fori_loop(0, 9, visit, 0)
            for axis in range(3):
                out_ref[axis, mine_l : mine_l + 1, :] = jnp.sum(
                    sum_ref[axis], axis=0, keepdims=True
                )


def total_field(far_ref, near_ref, moment, axis):
    field = near_ref[axis] + SELF_GAIN * moment

    def add(d, carry):
        return carry + far_ref[d, axis]

    return field + lax.fori_loop(0, far_ref.shape[0], add, jnp.zeros_like(moment), unroll=8)


def middle_kernel(where_ref, cot_ref, gain_ref, moment_ref, near_ref, far_ref, send_ref):
    cells_x = cot_ref.shape[1]
    devices = far_ref.shape[0]
    gain = gain_ref[...]
    parts = []
    for axis in range(3):
        field = total_field(far_ref, near_ref, moment_ref[where_ref[2], axis], axis)
        cot = jnp.concatenate([cot_ref[axis, cx] for cx in range(cells_x)], axis=0)
        parts.append(gain * (cot + field))
    block = jnp.stack(parts, axis=0)

    def put(d, carry):
        send_ref[d] = block
        return carry

    lax.fori_loop(0, devices, put, 0)


def last_kernel(where_ref, cot_ref, gain_ref, moment_ref, near_ref, far_ref, out_ref):
    cells_x, cells_y = cot_ref.shape[1:3]
    gain = gain_ref[...]
    for axis in range(3):
        field = total_field(far_ref, near_ref, moment_ref[where_ref[2], axis], axis)
        for cx in range(cells_x):
            rows = slice(cx * cells_y, (cx + 1) * cells_y)
            out_ref[axis, cx] = gain[rows] * (cot_ref[axis, cx] + field[rows])


def in_vmem(count, smem_first=False):
    specs = [pl.BlockSpec(memory_space=pltpu.VMEM)] * count
    if smem_first:
        specs[0] = pl.BlockSpec(memory_space=pltpu.SMEM)
    return specs


def call(body, outs, ins, scratch=(), smem_first=False, flops=1000):
    many = isinstance(outs, (list, tuple))
    out_specs = [pl.BlockSpec(memory_space=pltpu.VMEM)] * len(outs) if many else pl.BlockSpec(
        memory_space=pltpu.VMEM
    )
    return pl.pallas_call(
        body,
        out_shape=outs,
        in_specs=in_vmem(len(ins), smem_first),
        out_specs=out_specs,
        scratch_shapes=list(scratch),
        compiler_params=pltpu.CompilerParams(vmem_limit_bytes=VMEM_LIMIT),
        cost_estimate=pl.CostEstimate(flops=flops, bytes_accessed=100000, transcendentals=0),
    )(*ins)


def green_values(grid_x, grid_y, grid_z, length_x, length_y, length_z):
    def part(grid, length):
        signed = jnp.where(2 * grid < length, grid, grid - length).astype(F32) / length
        angle = 2.0 * math.pi / length * grid.astype(F32)
        factor = 9.0 / ((2.0 + jnp.cos(angle)) * (2.0 + jnp.cos(angle)))
        return (signed * signed, factor)

    square_x, factor_x = part(grid_x, length_x)
    square_y, factor_y = part(grid_y, length_y)
    square_z, factor_z = part(grid_z, length_z)
    square = square_x + square_y + square_z
    anchor = (grid_x == 0) & (grid_y == 0) & (grid_z == 0)
    safe = jnp.where(anchor, 1.0, square)
    value = jnp.exp(-(math.pi / BETA) * (math.pi / BETA) * safe) / (math.pi * safe)
    value = value * factor_x * factor_y * factor_z / (length_x * length_y * length_z)
    return jnp.where(anchor | (grid_z >= length_z), 0.0, value)


def shards(cotangent, polarizability, site_offset, site_fraction, cell_count):
    _, cells_x, cells_y, lanes = cotangent.shape
    layers = cell_count.shape[2]
    devices_x = lax.axis_size("gx")
    devices_y = lax.axis_size("gy")
    devices = devices_x * devices_y
    columns = cells_x * cells_y
    total_x = devices_x * cells_x
    length_x = total_x * HX
    length_y = devices_y * cells_y * HY
    length_z = layers * HZ
    index_x = lax.axis_index("gx")
    index_y = lax.axis_index("gy")
    me = index_x * devices_y + index_y
    where = jnp.stack([index_x, index_y, me]).astype(jnp.int32)

    def exchange(value):
        return lax.all_to_all(value, AXES, split_axis=0, concat_axis=0, tiled=True)

    send, gain = call(
        pack_kernel,
        [
            jax.ShapeDtypeStruct((devices, 7, columns, lanes), F32),
            jax.ShapeDtypeStruct((columns, lanes), F32),
        ],
        [cotangent, polarizability, site_offset, site_fraction, cell_count],
    )
    static = exchange(send)

    modes = me * MODES + jnp.arange(MODES, dtype=jnp.int32)
    mode_rows = jnp.broadcast_to(modes[:, None], (MODES, lanes))
    order = jnp.arange(4, dtype=jnp.int32)[:, None]
    angle = (2.0 * math.pi / length_z) * (modes[None, :] * order % length_z).astype(F32)
    phase = jnp.concatenate(
        [jnp.cos(angle) + jnp.sin(angle), jnp.cos(angle) - jnp.sin(angle)], axis=0
    )
    phase = jnp.broadcast_to(phase[:, :, None], (8, MODES, lanes))
    green = green_values(
        jnp.arange(length_x, dtype=jnp.int32)[None, None, :],
        jnp.arange(length_y, dtype=jnp.int32)[None, :, None],
        modes[:, None, None],
        length_x,
        length_y,
        length_z,
    ).reshape(MODES * length_y, length_x)
    forward, inverse = x_tables(total_x, length_x)
    y_high, y_low = two_terms(cas_table(length_y))
    y_table = np.concatenate([y_high, y_low, y_high], axis=1)

    tall = length_y * MODES
    kept = devices if devices * columns <= 256 else 1
    far_scratch = [
        pltpu.VMEM((total_x // 4, tall + 3 * MODES, 4 * 2 * SPAN), F32),
        pltpu.VMEM((length_x // 128, tall, 128), F32),
        pltpu.VMEM((length_x // 128, tall, 128), F32),
        pltpu.VMEM((total_x // 2, tall + 32, 2 * 4 * SPAN), BF16),
        pltpu.VMEM((kept, columns, 2 * SPAN, 2 * lanes), BF16),
        pltpu.VMEM((kept, columns, 2 * SPAN, lanes), F32),
        pltpu.VMEM((kept, columns, 2 * MODES, lanes), F32),
    ]
    far = functools.partial(far_kernel, (devices_x, devices_y, cells_x, cells_y, length_z))
    near = functools.partial(near_kernel, (devices_x, devices_y, cells_x, cells_y))
    near_scratch = [
        pltpu.VMEM(((cells_x + 2) * (cells_y + 2) * 7 * A, lanes), F32),
        pltpu.VMEM(((cells_x + 2) * (cells_y + 2), 7, A, lanes), F32),
        pltpu.VMEM((3, A, lanes), F32),
    ]
    moment = static[:, 3:6]
    for turn in range(ITERS):
        partial = call(
            far,
            jax.ShapeDtypeStruct((devices, 3, columns, lanes), F32),
            [
                static,
                moment,
                mode_rows,
                phase,
                green,
                *(jnp.asarray(t) for t in forward),
                *(jnp.asarray(t) for t in inverse),
                jnp.asarray(y_table),
            ],
            far_scratch,
            flops=10**9,
        )
        partial = exchange(partial)
        close = call(
            near,
            jax.ShapeDtypeStruct((3, columns, lanes), F32),
            [where, static, moment],
            near_scratch,
            smem_first=True,
            flops=10**8,
        )
        ins = [where, cotangent, gain, moment, close, partial]
        if turn < ITERS - 1:
            send = call(
                middle_kernel,
                jax.ShapeDtypeStruct((devices, 3, columns, lanes), F32),
                ins,
                smem_first=True,
            )
            moment = exchange(send)
        else:
            moment = call(
                last_kernel,
                jax.ShapeDtypeStruct(cotangent.shape, F32),
                ins,
                smem_first=True,
            )
    return moment


def solution(mesh):
    return jax.shard_map(
        shards,
        mesh=mesh,
        in_specs=(
            P(None, "gx", "gy", None),
            P("gx", "gy", None),
            P(None, "gx", "gy", None),
            P(None, "gx", "gy", None),
            P("gx", "gy", None),
        ),
        out_specs=P(None, "gx", "gy", None),
        check_vma=False,
    )
```

```python
import functools
import math

import jax
import jax.numpy as jnp
import ml_dtypes
import numpy as np
from jax import lax
from jax.experimental import pallas as pl
from jax.experimental.pallas import tpu as pltpu
from jax.sharding import PartitionSpec as P

A = 8
HX = 8
HY = 8
HZ = 16
ITERS = 2
BETA = 0.7
THOLE = 0.39
ROOT_PI = 1.7724538509055159
SELF_GAIN = 4.0 * BETA * BETA * BETA / (3.0 * ROOT_PI)
MODES = 8
STATIC_UNROLL = 2
SPAN = 16
AXES = ("gx", "gy")
F32 = jnp.float32
BF16 = jnp.bfloat16
MIB = 1024 * 1024


def two_terms(table):
    high = table.astype(ml_dtypes.bfloat16)
    low = (table - high.astype(np.float64)).astype(ml_dtypes.bfloat16)
    return high, low


def cas_table(length):
    grid = np.arange(length, dtype=np.int64)
    angle = 2.0 * np.pi / length * (grid[:, None] * grid[None, :] % length)
    return np.cos(angle) + np.sin(angle)


def x_tables(cells, length):
    cas = cas_table(length)
    place = (np.arange(cells)[:, None] * HX + np.arange(SPAN)[None, :]) % length
    forward = np.broadcast_to(cas[place][:, None], (cells, 2, SPAN, length))
    forward = forward.reshape(cells // 4, 4 * 2 * SPAN, length)
    inverse = np.broadcast_to(cas[place][:, None], (cells, 4, SPAN, length))
    inverse = inverse.reshape(cells // 2, 2 * 4 * SPAN, length).transpose(0, 2, 1)
    return two_terms(forward), two_terms(inverse)


def split(value):
    high = value.astype(BF16)
    low = (value - high.astype(F32)).astype(BF16)
    return high, low


def dot(left, right):
    return jnp.dot(left, right, preferred_element_type=F32)


def dot_nt(left, right):
    return lax.dot_general(left, right, (((1,), (1,)), ((), ())), preferred_element_type=F32)


def spline(fraction):
    rest = 1.0 - fraction
    square = fraction * fraction
    cube = square * fraction
    values = (
        rest * rest * rest / 6.0,
        (3.0 * cube - 6.0 * square + 4.0) / 6.0,
        (-3.0 * cube + 3.0 * square + 3.0 * fraction + 1.0) / 6.0,
        cube / 6.0,
    )
    slopes = (
        -0.5 * rest * rest,
        0.5 * (3.0 * square - 4.0 * fraction),
        0.5 * (-3.0 * square + 2.0 * fraction + 1.0),
        0.5 * square,
    )
    return values, slopes


def basis(anchor, weights):
    lanes = anchor.shape[1]
    index = lax.broadcasted_iota(jnp.int32, (SPAN, lanes), 0) - anchor
    total = jnp.zeros((SPAN, lanes), F32)
    for order in range(4):
        total = jnp.where(index == order, weights[order], total)
    return total


def turns(count, length):
    part = count.astype(F32) * (1.0 / length)
    half = math.pi * jnp.where(2 * count >= length, part - 1.0, part)
    square = half * half
    sine = 1.0
    for order in (10, 8, 6, 4, 2):
        sine = 1.0 - square * sine * (1.0 / (order * (order + 1)))
    sine = sine * half
    cosine = 1.0
    for order in (11, 9, 7, 5, 3, 1):
        cosine = 1.0 - square * cosine * (1.0 / (order * (order + 1)))
    return 1.0 - 2.0 * sine * sine, 2.0 * sine * cosine


def pack_kernel(cot_ref, polar_ref, offset_ref, fraction_ref, count_ref, send_ref, gain_ref, own_ref):
    cells_x, cells_y, lanes = polar_ref.shape
    devices = send_ref.shape[0]
    cells = lanes // A
    row = lax.broadcasted_iota(jnp.int32, (cells, lanes), 0)
    lane = lax.broadcasted_iota(jnp.int32, (cells, lanes), 1)
    widen = jnp.where(lane // A == row, 1.0, 0.0)
    slot = (lax.broadcasted_iota(jnp.int32, (cells_y, lanes), 1) % A).astype(F32)
    rows = [[] for _ in range(7)]
    gains = []
    for cx in range(cells_x):
        count = dot(count_ref[cx].astype(F32), widen)
        gain = jnp.where(slot < count, polar_ref[cx], 0.0)
        gains.append(gain)
        for axis in range(3):
            place = offset_ref[axis, cx].astype(F32) + 1.0 + fraction_ref[axis, cx]
            rows[axis].append(place)
            rows[3 + axis].append(gain * cot_ref[axis, cx])
        rows[6].append(polar_ref[cx])
    gain_ref[...] = jnp.concatenate(gains, axis=0)
    block = jnp.stack([jnp.concatenate(parts, axis=0) for parts in rows], axis=0)
    own_ref[...] = block[3:6]

    def put(d, carry):
        send_ref[d] = block
        return carry

    lax.fori_loop(0, devices, put, 0)


def far_kernel(
    shape,
    lead,
    where_ref,
    place_ref,
    moment_ref,
    green_ref,
    fx_high_ref,
    fx_low_ref,
    ix_high_ref,
    ix_low_ref,
    y_ref,
    out_ref,
    cell_ref,
    line_ref,
    wave_ref,
    side_ref,
    rise_ref,
    edge_ref,
):
    devices_x, devices_y, cells_x, cells_y, points_z = shape
    columns = cells_x * cells_y
    lanes = place_ref.shape[3]
    length_x = green_ref.shape[1]
    length_y = y_ref.shape[0]
    tall = length_y * MODES
    spill = 3 * MODES
    reach = (HY + 3) * MODES
    per_cell = HY * MODES
    turn_x = 4 // cells_x
    keep = side_ref.shape[0] > 1
    unroll = min(4, devices_y)
    layer = (lax.broadcasted_iota(jnp.int32, (1, lanes), 1) // A) * HZ
    mode = where_ref[2] * MODES + lax.broadcasted_iota(jnp.int32, (MODES, lanes), 0)
    plus, minus = [], []
    for order in range(4):
        cosine, sine = turns(lax.rem(mode * order, points_z), points_z)
        plus.append(cosine + sine)
        minus.append(cosine - sine)
    cell_ref[...] = jnp.zeros_like(cell_ref)

    def statics(d):
        k = d if keep else 0
        place = [place_ref[d, axis] for axis in range(3)]
        whole = [jnp.floor(value) for value in place]
        parts = [spline(value - low) for value, low in zip(place, whole)]
        anchors = [low.astype(jnp.int32) - 1 for low in whole]
        for l in range(columns):
            row = slice(l, l + 1)
            anchor = [value[row] for value in anchors]
            weights = [[[v[row] for v in kind] for kind in part] for part in parts]
            slopes_x = basis(anchor[0], weights[0][1])
            values_x = basis(anchor[0], weights[0][0])
            side = jnp.concatenate([slopes_x, values_x], axis=1)
            high, low = split(side)
            side_ref[k, l] = jnp.concatenate([high, low], axis=0)
            rise_ref[k, l] = jnp.concatenate(
                [basis(anchor[1], weights[1][0]), basis(anchor[1], weights[1][1])], axis=0
            )
            cosine, sine = turns(lax.rem(mode * (anchor[2] + layer), points_z), points_z)
            found = []
            for kind in weights[2]:
                up = kind[0] * plus[0]
                down = kind[0] * minus[0]
                for order in range(1, 4):
                    up = up + kind[order] * plus[order]
                    down = down + kind[order] * minus[order]
                found.append(cosine * up + sine * down)
            edge_ref[k, l] = jnp.concatenate(found, axis=0)

    def spread(d, l, slot, group, start):
        k = d if keep else 0
        first = edge_ref[k, l, :MODES] * moment_ref[d, lead, l : l + 1, :]
        second = edge_ref[k, l, :MODES] * moment_ref[d, lead + 1, l : l + 1, :]
        third = edge_ref[k, l, MODES:] * moment_ref[d, lead + 2, l : l + 1, :]
        tiles = []
        for y in range(HY + 3):
            value = rise_ref[k, l, y : y + 1, :]
            slope = rise_ref[k, l, SPAN + y : SPAN + y + 1, :]
            tile = jnp.concatenate([value * first, slope * second + value * third], axis=1)
            rest = tile - tile.astype(BF16).astype(F32)
            tiles.append(jnp.concatenate([tile, rest], axis=0).astype(BF16))
        sums = jnp.concatenate(tiles, axis=0)
        pieces = []
        if slot:
            pieces.append(jnp.zeros((slot * 2 * SPAN, 2 * lanes), BF16))
        pieces.append(side_ref[k, l])
        if slot < 3:
            pieces.append(jnp.zeros(((3 - slot) * 2 * SPAN, 2 * lanes), BF16))
        got = dot_nt(sums, jnp.concatenate(pieces, axis=0))
        got = got.reshape(HY + 3, 2, MODES, got.shape[1])
        got = (got[:, 0] + got[:, 1]).reshape(reach, got.shape[3])
        cell_ref[group, pl.ds(start, reach), :] = cell_ref[group, pl.ds(start, reach), :] + got

    def prepare(d, carry):
        statics(d)
        return carry

    if keep:
        lax.fori_loop(0, devices_x * devices_y, prepare, 0, unroll=STATIC_UNROLL)

    def spread_row(pair, carry):
        for odd in range(turn_x):
            gx = pair * turn_x + odd

            def spread_device(gy, inner):
                d = gx * devices_y + gy
                if not keep:
                    statics(d)
                for l in range(columns):
                    slot = odd * cells_x + l // cells_y
                    start = pl.multiple_of(
                        (gy * cells_y + l % cells_y) * per_cell, per_cell
                    )
                    spread(d, l, slot, pair, start)
                return inner

            lax.fori_loop(0, devices_y, spread_device, 0, unroll=unroll)
        return carry

    lax.fori_loop(0, devices_x // turn_x, spread_row, 0)

    cell_ref[:, :spill, :] = cell_ref[:, :spill, :] + cell_ref[:, tall : tall + spill, :]
    total = jnp.zeros((tall, length_x), F32)
    for group in range(0, cell_ref.shape[0], 2):
        one_high, one_low = split(cell_ref[group, :tall, :])
        two_high, two_low = split(cell_ref[group + 1, :tall, :])
        one, two = fx_high_ref[group], fx_high_ref[group + 1]
        total = total + dot(
            jnp.concatenate([one_high, one_low], axis=1), jnp.concatenate([one, one], axis=0)
        )
        total = total + dot(
            jnp.concatenate([two_high, two_low], axis=1), jnp.concatenate([two, two], axis=0)
        )
        total = total + dot(
            jnp.concatenate([one_high, two_high], axis=1),
            jnp.concatenate([fx_low_ref[group], fx_low_ref[group + 1]], axis=0),
        )
    blocks = length_x // line_ref.shape[2]
    width = line_ref.shape[2]
    for block in range(blocks):
        line_ref[block] = total[:, block * width : (block + 1) * width]

    def along_y(value):
        high, low = split(value)
        return dot(y_ref[...], jnp.concatenate([high, high, low], axis=0))

    for block in range(blocks):
        found = []
        for number in range(MODES):
            got = along_y(line_ref[block, pl.ds(number, length_y, stride=MODES), :])
            found.append(
                got
                * green_ref[
                    number * length_y : (number + 1) * length_y,
                    block * width : (block + 1) * width,
                ]
            )
        for number in range(MODES):
            line_ref[block, pl.ds(number, length_y, stride=MODES), :] = along_y(found[number])
    high, low = split(jnp.concatenate([line_ref[block] for block in range(blocks)], axis=1))
    both = jnp.concatenate([high, low], axis=1)
    lane = lax.broadcasted_iota(jnp.int32, (tall, 4 * 4 * SPAN), 1)
    rest = lane // SPAN % 2 == 1
    for group in range(0, wave_ref.shape[0], 2):
        one = jnp.concatenate([ix_high_ref[group], ix_high_ref[group + 1]], axis=1)
        two = jnp.concatenate([ix_low_ref[group], ix_low_ref[group + 1]], axis=1)
        got = dot(both, jnp.concatenate([one, one], axis=0)) + dot(high, two)
        got = jnp.where(rest, got - got.astype(BF16).astype(F32), got).astype(BF16)
        for odd in range(2):
            part = got[:, odd * 8 * SPAN : (odd + 1) * 8 * SPAN]
            wave_ref[group + odd, :tall, :] = part
            wave_ref[group + odd, tall:, :] = part[: wave_ref.shape[1] - tall]

    window = -(-reach // 16) * 16

    def gather(d, l, slot, group, start):
        k = d if keep else 0
        high = side_ref[k, l, :SPAN]
        low = side_ref[k, l, SPAN:]
        block = [high, high, low, low]
        zero = jnp.zeros((4 * SPAN, 2 * lanes), BF16)
        pieces = [zero] + block if slot else block + [zero]
        got = dot(wave_ref[group, pl.ds(start, window), :], jnp.concatenate(pieces, axis=0))
        sums = [jnp.zeros((MODES, lanes), F32) for _ in range(3)]
        for y in range(HY + 3):
            value = rise_ref[k, l, y : y + 1, :]
            slope = rise_ref[k, l, SPAN + y : SPAN + y + 1, :]
            sloped = got[y * MODES : (y + 1) * MODES, :lanes]
            plain = got[y * MODES : (y + 1) * MODES, lanes:]
            sums[0] = sums[0] + sloped * value
            sums[1] = sums[1] + plain * slope
            sums[2] = sums[2] + plain * value
        value = edge_ref[k, l, :MODES]
        slope = edge_ref[k, l, MODES:]
        return [
            -jnp.sum(sums[axis] * part, axis=0, keepdims=True)
            for axis, part in enumerate((value, value, slope))
        ]

    def gather_row(gx, carry):
        def gather_device(gy, inner):
            d = gx * devices_y + gy
            if not keep:
                statics(d)
            found = []
            for l in range(columns):
                across = l // cells_y
                start = pl.multiple_of((gy * cells_y + l % cells_y) * per_cell, per_cell)
                group = (gx * cells_x + across - across % 2) // 2
                found.append(gather(d, l, across % 2, group, start))
            for axis in range(3):
                out_ref[d, axis] = jnp.concatenate([part[axis] for part in found], axis=0)
            return inner

        lax.fori_loop(0, devices_y, gather_device, 0, unroll=unroll)
        return carry

    lax.fori_loop(0, devices_x, gather_row, 0)


def near_kernel(shape, lead, where_ref, static_ref, moment_ref, out_ref, raw_ref, wide_ref, sum_ref):
    devices_x, devices_y, cells_x, cells_y = shape
    lanes = static_ref.shape[3]
    rows_x, rows_y = cells_x + 2, cells_y + 2
    total_x, total_y = devices_x * cells_x, devices_y * cells_y
    lane = lax.broadcasted_iota(jnp.int32, (A, lanes), 1)
    sub = lax.broadcasted_iota(jnp.int32, (A, lanes), 0)
    own = lane % A == sub
    for a in range(rows_x):
        for b in range(rows_y):
            cell_x = lax.rem(where_ref[0] * cells_x + (a - 1 + total_x), total_x)
            cell_y = lax.rem(where_ref[1] * cells_y + (b - 1 + total_y), total_y)
            d = (cell_x // cells_x) * devices_y + cell_y // cells_y
            l = lax.rem(cell_x, cells_x) * cells_y + lax.rem(cell_y, cells_y)
            for item in range(7):
                if item < 4:
                    row = static_ref[d, item if item < 3 else 6, pl.ds(l, 1), :]
                else:
                    row = moment_ref[d, lead + item - 4, pl.ds(l, 1), :]
                first = ((a * rows_y + b) * 7 + item) * A
                raw_ref[first : first + A, :] = jnp.where(own, row, 0.0)
    group = lax.broadcasted_iota(jnp.int32, (lanes, lanes), 0) // A
    other = lax.broadcasted_iota(jnp.int32, (lanes, lanes), 1) // A
    ones = jnp.where(group == other, 1.0, 0.0).astype(BF16)
    raw = raw_ref[...]
    high = raw.astype(BF16)
    raw = raw - high.astype(F32)
    middle = raw.astype(BF16)
    low = (raw - middle.astype(F32)).astype(BF16)
    wide = dot(low, ones) + dot(middle, ones) + dot(high, ones)
    wide_ref[...] = wide.reshape(wide_ref.shape)

    for across in range(cells_x):
        for along in range(cells_y):
            mine = (across + 1) * rows_y + along + 1
            mine_d = where_ref[0] * devices_y + where_ref[1]
            mine_l = across * cells_y + along
            at = [static_ref[mine_d, axis, mine_l : mine_l + 1, :] for axis in range(3)]
            polar = static_ref[mine_d, 6, mine_l : mine_l + 1, :]
            sum_ref[...] = jnp.zeros_like(sum_ref)

            def visit(step, carry, across=across, along=along, at=at, polar=polar):
                dx = step // 3 - 1
                dy = lax.rem(step, 3) - 1
                found = (across + 1 + dx) * rows_y + along + 1 + dy
                shift_x = dx.astype(F32) * HX
                shift_y = dy.astype(F32) * HY
                sums = [sum_ref[axis] for axis in range(3)]
                for dz in (-1, 0, 1):
                    near = [wide_ref[found, item] for item in range(7)]
                    if dz:
                        near = [pltpu.roll(v, (-dz * A) % lanes, 1) for v in near]
                    r0 = at[0] - near[0] - shift_x
                    r1 = at[1] - near[1] - shift_y
                    r2 = at[2] - near[2] - float(dz * HZ)
                    square = r0 * r0 + r1 * r1 + r2 * r2
                    if dz == 0:
                        selfish = own & (step == 4)
                        square = jnp.where(selfish, 1.0, square)
                    inverse = lax.rsqrt(square)
                    inverse_square = inverse * inverse
                    distance = square * inverse
                    root_inverse = lax.rsqrt(polar * near[3])
                    t = 1.0 / (1.0 + (0.5 * BETA) * distance)
                    series = 0.17087277
                    for c in (-0.82215223, 1.48851587, -1.13520398, 0.27886807,
                              -0.18628806, 0.09678418, 0.37409196, 1.00002368, -1.26551223):
                        series = series * t + c
                    bell = jnp.exp((-BETA * BETA) * square)
                    screened = t * jnp.exp(series) * bell * inverse
                    gauss = (2.0 * BETA / ROOT_PI) * bell
                    first = (screened + gauss) * inverse_square
                    second = (3.0 * first + (2.0 * BETA * BETA) * gauss) * inverse_square
                    scaled = THOLE * square * distance * root_inverse
                    damping = jnp.exp(-scaled) * (inverse_square * inverse)
                    first = first - damping
                    second = second - 3.0 * (1.0 + scaled) * damping * inverse_square
                    if dz == 0:
                        first = jnp.where(selfish, 0.0, first)
                        second = jnp.where(selfish, 0.0, second)
                    projected = second * (r0 * near[4] + r1 * near[5] + r2 * near[6])
                    sums[0] = sums[0] + (projected * r0 - first * near[4])
                    sums[1] = sums[1] + (projected * r1 - first * near[5])
                    sums[2] = sums[2] + (projected * r2 - first * near[6])
                for axis in range(3):
                    sum_ref[axis] = sums[axis]
                return carry

            lax.fori_loop(0, 9, visit, 0)
            for axis in range(3):
                out_ref[axis, mine_l : mine_l + 1, :] = jnp.sum(
                    sum_ref[axis], axis=0, keepdims=True
                )


def total_field(far_ref, near_ref, moment, axis):
    field = near_ref[axis] + SELF_GAIN * moment

    def add(d, carry):
        return carry + far_ref[d, axis]

    return field + lax.fori_loop(0, far_ref.shape[0], add, jnp.zeros_like(moment), unroll=8)


def middle_kernel(cot_ref, gain_ref, moment_ref, near_ref, far_ref, send_ref, own_ref):
    cells_x = cot_ref.shape[1]
    devices = far_ref.shape[0]
    gain = gain_ref[...]
    parts = []
    for axis in range(3):
        field = total_field(far_ref, near_ref, moment_ref[axis], axis)
        cot = jnp.concatenate([cot_ref[axis, cx] for cx in range(cells_x)], axis=0)
        parts.append(gain * (cot + field))
    block = jnp.stack(parts, axis=0)
    own_ref[...] = block

    def put(d, carry):
        send_ref[d] = block
        return carry

    lax.fori_loop(0, devices, put, 0)


def last_kernel(cot_ref, gain_ref, moment_ref, near_ref, far_ref, out_ref):
    cells_x, cells_y = cot_ref.shape[1:3]
    gain = gain_ref[...]
    for axis in range(3):
        field = total_field(far_ref, near_ref, moment_ref[axis], axis)
        for cx in range(cells_x):
            rows = slice(cx * cells_y, (cx + 1) * cells_y)
            out_ref[axis, cx] = gain[rows] * (cot_ref[axis, cx] + field[rows])


def in_vmem(count, smem_first=False):
    specs = [pl.BlockSpec(memory_space=pltpu.VMEM)] * count
    if smem_first:
        specs[0] = pl.BlockSpec(memory_space=pltpu.SMEM)
    return specs


def call(body, outs, ins, scratch=(), smem_first=False, flops=1000, limit=12):
    many = isinstance(outs, (list, tuple))
    out_specs = [pl.BlockSpec(memory_space=pltpu.VMEM)] * len(outs) if many else pl.BlockSpec(
        memory_space=pltpu.VMEM
    )
    return pl.pallas_call(
        body,
        out_shape=outs,
        in_specs=in_vmem(len(ins), smem_first),
        out_specs=out_specs,
        scratch_shapes=list(scratch),
        compiler_params=pltpu.CompilerParams(vmem_limit_bytes=limit * MIB),
        cost_estimate=pl.CostEstimate(flops=flops, bytes_accessed=100000, transcendentals=0),
    )(*ins)


def green_values(grid_x, grid_y, grid_z, length_x, length_y, length_z):
    def part(grid, length):
        signed = jnp.where(2 * grid < length, grid, grid - length).astype(F32) / length
        angle = 2.0 * math.pi / length * grid.astype(F32)
        factor = 9.0 / ((2.0 + jnp.cos(angle)) * (2.0 + jnp.cos(angle)))
        return (signed * signed, factor)

    square_x, factor_x = part(grid_x, length_x)
    square_y, factor_y = part(grid_y, length_y)
    square_z, factor_z = part(grid_z, length_z)
    square = square_x + square_y + square_z
    anchor = (grid_x == 0) & (grid_y == 0) & (grid_z == 0)
    safe = jnp.where(anchor, 1.0, square)
    value = jnp.exp(-(math.pi / BETA) * (math.pi / BETA) * safe) / (math.pi * safe)
    value = value * factor_x * factor_y * factor_z / (length_x * length_y * length_z)
    return jnp.where(anchor | (grid_z >= length_z), 0.0, value)


def shards(cotangent, polarizability, site_offset, site_fraction, cell_count):
    _, cells_x, cells_y, lanes = cotangent.shape
    layers = cell_count.shape[2]
    devices_x = lax.axis_size("gx")
    devices_y = lax.axis_size("gy")
    devices = devices_x * devices_y
    columns = cells_x * cells_y
    total_x = devices_x * cells_x
    length_x = total_x * HX
    length_y = devices_y * cells_y * HY
    length_z = layers * HZ
    index_x = lax.axis_index("gx")
    index_y = lax.axis_index("gy")
    me = index_x * devices_y + index_y
    where = jnp.stack([index_x, index_y, me]).astype(jnp.int32)

    def exchange(value):
        return lax.all_to_all(value, AXES, split_axis=0, concat_axis=0, tiled=True)

    own_shape = jax.ShapeDtypeStruct((3, columns, lanes), F32)
    moment_shape = jax.ShapeDtypeStruct((devices, 3, columns, lanes), F32)
    send, gain, own = call(
        pack_kernel,
        [
            jax.ShapeDtypeStruct((devices, 7, columns, lanes), F32),
            jax.ShapeDtypeStruct((columns, lanes), F32),
            own_shape,
        ],
        [cotangent, polarizability, site_offset, site_fraction, cell_count],
        limit=58,
    )
    static = exchange(send)

    modes = me * MODES + jnp.arange(MODES, dtype=jnp.int32)
    green = green_values(
        jnp.arange(length_x, dtype=jnp.int32)[None, None, :],
        jnp.arange(length_y, dtype=jnp.int32)[None, :, None],
        modes[:, None, None],
        length_x,
        length_y,
        length_z,
    ).reshape(MODES * length_y, length_x)
    forward, inverse = x_tables(total_x, length_x)
    y_high, y_low = two_terms(cas_table(length_y))
    y_table = np.concatenate([y_high, y_low, y_high], axis=1)

    tall = length_y * MODES
    kept = devices if devices * columns <= 256 else 1
    far_scratch = [
        pltpu.VMEM((total_x // 4, tall + 3 * MODES, 4 * 2 * SPAN), F32),
        pltpu.VMEM((length_x // 128, tall, 128), F32),
        pltpu.VMEM((total_x // 2, tall + 32, 2 * 4 * SPAN), BF16),
        pltpu.VMEM((kept, columns, 2 * SPAN, 2 * lanes), BF16),
        pltpu.VMEM((kept, columns, 2 * SPAN, lanes), F32),
        pltpu.VMEM((kept, columns, 2 * MODES, lanes), F32),
    ]
    far_shape = (devices_x, devices_y, cells_x, cells_y, length_z)
    near_shape = (devices_x, devices_y, cells_x, cells_y)

    def far_first(where_ref, static_ref, *rest):
        far_kernel(far_shape, 3, where_ref, static_ref, static_ref, *rest)

    def near_first(where_ref, static_ref, *rest):
        near_kernel(near_shape, 3, where_ref, static_ref, static_ref, *rest)

    far_later = functools.partial(far_kernel, far_shape, 0)
    near_later = functools.partial(near_kernel, near_shape, 0)
    near_scratch = [
        pltpu.VMEM(((cells_x + 2) * (cells_y + 2) * 7 * A, lanes), F32),
        pltpu.VMEM(((cells_x + 2) * (cells_y + 2), 7, A, lanes), F32),
        pltpu.VMEM((3, A, lanes), F32),
    ]
    tables = [green, *(jnp.asarray(t) for t in (*forward, *inverse, y_table))]
    data = [where, static]
    for turn in range(ITERS):
        partial = call(
            far_later if turn else far_first,
            moment_shape,
            data + tables,
            far_scratch,
            smem_first=True,
            flops=10**9,
            limit=20 if kept > 1 else 58,
        )
        partial = exchange(partial)
        close = call(
            near_later if turn else near_first,
            own_shape,
            data,
            near_scratch,
            smem_first=True,
            flops=10**8,
        )
        ins = [cotangent, gain, own, close, partial]
        if turn < ITERS - 1:
            send, own = call(middle_kernel, [moment_shape, own_shape], ins)
            data = [where, static, exchange(send)]
        else:
            moment = call(last_kernel, jax.ShapeDtypeStruct(cotangent.shape, F32), ins)
    return moment


def solution(mesh):
    return jax.shard_map(
        shards,
        mesh=mesh,
        in_specs=(
            P(None, "gx", "gy", None),
            P("gx", "gy", None),
            P(None, "gx", "gy", None),
            P(None, "gx", "gy", None),
            P("gx", "gy", None),
        ),
        out_specs=P(None, "gx", "gy", None),
        check_vma=False,
    )
```

```python
import functools
import math

import jax
import jax.numpy as jnp
import ml_dtypes
import numpy as np
from jax import lax
from jax.experimental import pallas as pl
from jax.experimental.pallas import tpu as pltpu
from jax.sharding import PartitionSpec as P

A = 8
HX = 8
HY = 8
HZ = 16
ITERS = 2
BETA = 0.7
THOLE = 0.39
ROOT_PI = 1.7724538509055159
SELF_GAIN = 4.0 * BETA * BETA * BETA / (3.0 * ROOT_PI)
MODES = 8
STATIC_UNROLL = 8
SPAN = 16
AXES = ("gx", "gy")
F32 = jnp.float32
BF16 = jnp.bfloat16
MIB = 1024 * 1024


def two_terms(table):
    high = table.astype(ml_dtypes.bfloat16)
    low = (table - high.astype(np.float64)).astype(ml_dtypes.bfloat16)
    return high, low


def cas_table(length):
    grid = np.arange(length, dtype=np.int64)
    angle = 2.0 * np.pi / length * (grid[:, None] * grid[None, :] % length)
    return np.cos(angle) + np.sin(angle)


def x_tables(cells, length):
    cas = cas_table(length)
    place = (np.arange(cells)[:, None] * HX + np.arange(SPAN)[None, :]) % length
    forward = np.broadcast_to(cas[place][:, None], (cells, 2, SPAN, length))
    forward = forward.reshape(cells // 4, 4 * 2 * SPAN, length)
    inverse = np.broadcast_to(cas[place][:, None], (cells, 4, SPAN, length))
    inverse = inverse.reshape(cells // 2, 2 * 4 * SPAN, length).transpose(0, 2, 1)
    return two_terms(forward), two_terms(inverse)


def split(value):
    high = value.astype(BF16)
    low = (value - high.astype(F32)).astype(BF16)
    return high, low


def dot(left, right):
    return jnp.dot(left, right, preferred_element_type=F32)


def dot_nt(left, right):
    return lax.dot_general(left, right, (((1,), (1,)), ((), ())), preferred_element_type=F32)


def spline(fraction):
    rest = 1.0 - fraction
    square = fraction * fraction
    cube = square * fraction
    values = (
        rest * rest * rest / 6.0,
        (3.0 * cube - 6.0 * square + 4.0) / 6.0,
        (-3.0 * cube + 3.0 * square + 3.0 * fraction + 1.0) / 6.0,
        cube / 6.0,
    )
    slopes = (
        -0.5 * rest * rest,
        0.5 * (3.0 * square - 4.0 * fraction),
        0.5 * (-3.0 * square + 2.0 * fraction + 1.0),
        0.5 * square,
    )
    return values, slopes


def basis(anchor, weights):
    lanes = anchor.shape[1]
    index = lax.broadcasted_iota(jnp.int32, (SPAN, lanes), 0) - anchor
    total = jnp.zeros((SPAN, lanes), F32)
    for order in range(4):
        total = jnp.where(index == order, weights[order], total)
    return total


def turns(count, length):
    part = count.astype(F32) * (1.0 / length)
    half = math.pi * jnp.where(2 * count >= length, part - 1.0, part)
    square = half * half
    sine = 1.0
    for order in (10, 8, 6, 4, 2):
        sine = 1.0 - square * sine * (1.0 / (order * (order + 1)))
    sine = sine * half
    cosine = 1.0
    for order in (11, 9, 7, 5, 3, 1):
        cosine = 1.0 - square * cosine * (1.0 / (order * (order + 1)))
    return 1.0 - 2.0 * sine * sine, 2.0 * sine * cosine


def pack_kernel(cot_ref, polar_ref, offset_ref, fraction_ref, count_ref, send_ref, gain_ref, own_ref):
    cells_x, cells_y, lanes = polar_ref.shape
    devices = send_ref.shape[0]
    cells = lanes // A
    row = lax.broadcasted_iota(jnp.int32, (cells, lanes), 0)
    lane = lax.broadcasted_iota(jnp.int32, (cells, lanes), 1)
    widen = jnp.where(lane // A == row, 1.0, 0.0)
    slot = (lax.broadcasted_iota(jnp.int32, (cells_y, lanes), 1) % A).astype(F32)
    rows = [[] for _ in range(7)]
    gains = []
    for cx in range(cells_x):
        count = dot(count_ref[cx].astype(F32), widen)
        gain = jnp.where(slot < count, polar_ref[cx], 0.0)
        gains.append(gain)
        for axis in range(3):
            place = offset_ref[axis, cx].astype(F32) + 1.0 + fraction_ref[axis, cx]
            rows[axis].append(place)
            rows[3 + axis].append(gain * cot_ref[axis, cx])
        rows[6].append(polar_ref[cx])
    gain_ref[...] = jnp.concatenate(gains, axis=0)
    block = jnp.stack([jnp.concatenate(parts, axis=0) for parts in rows], axis=0)
    own_ref[...] = block[3:6]

    def put(d, carry):
        send_ref[d] = block
        return carry

    lax.fori_loop(0, devices, put, 0)


def far_kernel(
    shape,
    lead,
    where_ref,
    place_ref,
    moment_ref,
    green_ref,
    fx_high_ref,
    fx_low_ref,
    ix_high_ref,
    ix_low_ref,
    y_ref,
    out_ref,
    side_ref,
    form_ref,
    cell_ref,
    line_ref,
    wave_ref,
):
    edge = 2 * SPAN
    devices_x, devices_y, cells_x, cells_y, points_z = shape
    columns = cells_x * cells_y
    lanes = place_ref.shape[3]
    length_x = line_ref.shape[0] * line_ref.shape[2]
    tall = line_ref.shape[1]
    length_y = tall // MODES
    spill = 3 * MODES
    reach = (HY + 3) * MODES
    per_cell = HY * MODES
    turn_x = 4 // cells_x
    keep = form_ref.shape[0] > 1
    unroll = min(4, devices_y)
    layer = (lax.broadcasted_iota(jnp.int32, (1, lanes), 1) // A) * HZ
    mode = where_ref[2] * MODES + lax.broadcasted_iota(jnp.int32, (MODES, lanes), 0)
    plus, minus = [], []
    for order in range(4):
        cosine, sine = turns(lax.rem(mode * order, points_z), points_z)
        plus.append(cosine + sine)
        minus.append(cosine - sine)

    def statics(d):
        k = d if keep else 0
        place = [place_ref[d, axis] for axis in range(3)]
        whole = [jnp.floor(value) for value in place]
        parts = [spline(value - low) for value, low in zip(place, whole)]
        anchors = [low.astype(jnp.int32) - 1 for low in whole]
        for l in range(columns):
            row = slice(l, l + 1)
            anchor = [value[row] for value in anchors]
            weights = [[[v[row] for v in kind] for kind in part] for part in parts]
            slopes_x = basis(anchor[0], weights[0][1])
            values_x = basis(anchor[0], weights[0][0])
            high, low = split(jnp.concatenate([slopes_x, values_x], axis=1))
            side_ref[k, l] = jnp.concatenate([high, low], axis=0)
            form_ref[k, l, :edge] = jnp.concatenate(
                [basis(anchor[1], weights[1][0]), basis(anchor[1], weights[1][1])], axis=0
            )
            cosine, sine = turns(lax.rem(mode * (anchor[2] + layer), points_z), points_z)
            found = []
            for kind in weights[2]:
                up = kind[0] * plus[0]
                down = kind[0] * minus[0]
                for order in range(1, 4):
                    up = up + kind[order] * plus[order]
                    down = down + kind[order] * minus[order]
                found.append(cosine * up + sine * down)
            form_ref[k, l, edge:] = jnp.concatenate(found, axis=0)

    def spread_parts(d, l, slot):
        k = d if keep else 0
        first = form_ref[k, l, edge : edge + MODES] * moment_ref[d, lead, l : l + 1, :]
        second = form_ref[k, l, edge : edge + MODES] * moment_ref[d, lead + 1, l : l + 1, :]
        third = form_ref[k, l, edge + MODES :] * moment_ref[d, lead + 2, l : l + 1, :]
        tiles = []
        for y in range(HY + 3):
            value = form_ref[k, l, y : y + 1, :]
            slope = form_ref[k, l, SPAN + y : SPAN + y + 1, :]
            tile = jnp.concatenate([value * first, slope * second + value * third], axis=1)
            rest = tile - tile.astype(BF16).astype(F32)
            tiles.append(jnp.concatenate([tile, rest], axis=0).astype(BF16))
        pieces = []
        if slot:
            pieces.append(jnp.zeros((slot * 2 * SPAN, 2 * lanes), BF16))
        pieces.append(side_ref[k, l])
        if slot < 3:
            pieces.append(jnp.zeros(((3 - slot) * 2 * SPAN, 2 * lanes), BF16))
        return jnp.concatenate(tiles, axis=0), jnp.concatenate(pieces, axis=0)

    def prepare(d, carry):
        statics(d)
        return carry

    if keep:
        lax.fori_loop(0, devices_x * devices_y, prepare, 0, unroll=STATIC_UNROLL)

    def spread_row(pair, carry):
        def spread_device(gy, over):
            parts = [[] for _ in range(cells_y)]
            for odd in range(turn_x):
                d = (pair * turn_x + odd) * devices_y + gy
                if not keep:
                    statics(d)
                for l in range(columns):
                    left, right = spread_parts(d, l, odd * cells_x + l // cells_y)
                    parts[l % cells_y].append((left, right))
            for low in range(cells_y):
                start = pl.multiple_of((gy * cells_y + low) * per_cell, per_cell)
                left, right = (jnp.concatenate(part, axis=1) for part in zip(*parts[low]))
                got = dot_nt(left, right).reshape(HY + 3, 2, MODES, 8 * SPAN)
                got = (got[:, 0] + got[:, 1]).reshape(reach, 8 * SPAN)
                cell_ref[pair, pl.ds(start, spill), :] = got[:spill] + over
                cell_ref[pair, pl.ds(start + spill, per_cell - spill), :] = got[spill:per_cell]
                over = got[per_cell:]
            return over

        over = lax.fori_loop(
            0, devices_y, spread_device, jnp.zeros((spill, 8 * SPAN), F32), unroll=unroll
        )
        cell_ref[pair, :spill, :] = cell_ref[pair, :spill, :] + over
        return carry

    lax.fori_loop(0, devices_x // turn_x, spread_row, 0)

    total = jnp.zeros((tall, length_x), F32)
    for group in range(0, cell_ref.shape[0], 2):
        one_high, one_low = split(cell_ref[group])
        two_high, two_low = split(cell_ref[group + 1])
        one, two = fx_high_ref[group], fx_high_ref[group + 1]
        total = total + dot(
            jnp.concatenate([one_high, one_low], axis=1), jnp.concatenate([one, one], axis=0)
        )
        total = total + dot(
            jnp.concatenate([two_high, two_low], axis=1), jnp.concatenate([two, two], axis=0)
        )
        total = total + dot(
            jnp.concatenate([one_high, two_high], axis=1),
            jnp.concatenate([fx_low_ref[group], fx_low_ref[group + 1]], axis=0),
        )
    blocks = length_x // line_ref.shape[2]
    width = line_ref.shape[2]
    for block in range(blocks):
        line_ref[block] = total[:, block * width : (block + 1) * width]

    def along_y(value):
        high, low = split(value)
        return dot(y_ref[...], jnp.concatenate([high, high, low], axis=0))

    for block in range(blocks):
        found = []
        for number in range(MODES):
            got = along_y(line_ref[block, pl.ds(number, length_y, stride=MODES), :])
            found.append(
                got
                * green_ref[
                    number * length_y : (number + 1) * length_y,
                    block * width : (block + 1) * width,
                ]
            )
        for number in range(MODES):
            line_ref[block, pl.ds(number, length_y, stride=MODES), :] = along_y(found[number])
    high, low = split(jnp.concatenate([line_ref[block] for block in range(blocks)], axis=1))
    both = jnp.concatenate([high, low], axis=1)
    lane = lax.broadcasted_iota(jnp.int32, (tall, 4 * 4 * SPAN), 1)
    rest = lane // SPAN % 2 == 1
    for group in range(0, wave_ref.shape[0], 2):
        one = jnp.concatenate([ix_high_ref[group], ix_high_ref[group + 1]], axis=1)
        two = jnp.concatenate([ix_low_ref[group], ix_low_ref[group + 1]], axis=1)
        got = dot(both, jnp.concatenate([one, one], axis=0)) + dot(high, two)
        got = jnp.where(rest, got - got.astype(BF16).astype(F32), got).astype(BF16)
        for odd in range(2):
            part = got[:, odd * 8 * SPAN : (odd + 1) * 8 * SPAN]
            wave_ref[group + odd, :tall, :] = part
            wave_ref[group + odd, tall:, :] = part[: wave_ref.shape[1] - tall]

    window = -(-reach // 16) * 16

    def gather(d, l, slot, group, start):
        k = d if keep else 0
        found = side_ref[k, l]
        high, low = found[:SPAN], found[SPAN:]
        block = [high, high, low, low]
        zero = jnp.zeros((4 * SPAN, 2 * lanes), BF16)
        pieces = [zero] + block if slot else block + [zero]
        got = dot(wave_ref[group, pl.ds(start, window), :], jnp.concatenate(pieces, axis=0))
        sums = [jnp.zeros((MODES, lanes), F32) for _ in range(3)]
        for y in range(HY + 3):
            value = form_ref[k, l, y : y + 1, :]
            slope = form_ref[k, l, SPAN + y : SPAN + y + 1, :]
            sloped = got[y * MODES : (y + 1) * MODES, :lanes]
            plain = got[y * MODES : (y + 1) * MODES, lanes:]
            sums[0] = sums[0] + sloped * value
            sums[1] = sums[1] + plain * slope
            sums[2] = sums[2] + plain * value
        value = form_ref[k, l, edge : edge + MODES]
        slope = form_ref[k, l, edge + MODES :]
        return [
            -jnp.sum(sums[axis] * part, axis=0, keepdims=True)
            for axis, part in enumerate((value, value, slope))
        ]

    def gather_row(gx, carry):
        def gather_device(gy, inner):
            d = gx * devices_y + gy
            if not keep:
                statics(d)
            found = []
            for l in range(columns):
                across = l // cells_y
                start = pl.multiple_of((gy * cells_y + l % cells_y) * per_cell, per_cell)
                group = (gx * cells_x + across - across % 2) // 2
                found.append(gather(d, l, across % 2, group, start))
            for axis in range(3):
                out_ref[d, axis] = jnp.concatenate([part[axis] for part in found], axis=0)
            return inner

        lax.fori_loop(0, devices_y, gather_device, 0, unroll=unroll)
        return carry

    lax.fori_loop(0, devices_x, gather_row, 0)


def near_kernel(shape, lead, where_ref, static_ref, moment_ref, out_ref, raw_ref, wide_ref, sum_ref):
    devices_x, devices_y, cells_x, cells_y = shape
    lanes = static_ref.shape[3]
    rows_x, rows_y = cells_x + 2, cells_y + 2
    total_x, total_y = devices_x * cells_x, devices_y * cells_y
    lane = lax.broadcasted_iota(jnp.int32, (A, lanes), 1)
    sub = lax.broadcasted_iota(jnp.int32, (A, lanes), 0)
    own = lane % A == sub
    for a in range(rows_x):
        for b in range(rows_y):
            cell_x = lax.rem(where_ref[0] * cells_x + (a - 1 + total_x), total_x)
            cell_y = lax.rem(where_ref[1] * cells_y + (b - 1 + total_y), total_y)
            d = (cell_x // cells_x) * devices_y + cell_y // cells_y
            l = lax.rem(cell_x, cells_x) * cells_y + lax.rem(cell_y, cells_y)
            for item in range(7):
                if item < 4:
                    row = static_ref[d, item if item < 3 else 6, pl.ds(l, 1), :]
                else:
                    row = moment_ref[d, lead + item - 4, pl.ds(l, 1), :]
                first = ((a * rows_y + b) * 7 + item) * A
                raw_ref[first : first + A, :] = jnp.where(own, row, 0.0)
    group = lax.broadcasted_iota(jnp.int32, (lanes, lanes), 0) // A
    other = lax.broadcasted_iota(jnp.int32, (lanes, lanes), 1) // A
    ones = jnp.where(group == other, 1.0, 0.0).astype(BF16)
    raw = raw_ref[...]
    high = raw.astype(BF16)
    raw = raw - high.astype(F32)
    middle = raw.astype(BF16)
    low = (raw - middle.astype(F32)).astype(BF16)
    wide = dot(low, ones) + dot(middle, ones) + dot(high, ones)
    wide_ref[...] = wide.reshape(wide_ref.shape)

    for across in range(cells_x):
        for along in range(cells_y):
            mine = (across + 1) * rows_y + along + 1
            mine_d = where_ref[0] * devices_y + where_ref[1]
            mine_l = across * cells_y + along
            at = [static_ref[mine_d, axis, mine_l : mine_l + 1, :] for axis in range(3)]
            polar = static_ref[mine_d, 6, mine_l : mine_l + 1, :]
            sum_ref[...] = jnp.zeros_like(sum_ref)

            def visit(step, carry, across=across, along=along, at=at, polar=polar):
                dx = step // 3 - 1
                dy = lax.rem(step, 3) - 1
                found = (across + 1 + dx) * rows_y + along + 1 + dy
                shift_x = dx.astype(F32) * HX
                shift_y = dy.astype(F32) * HY
                sums = [sum_ref[axis] for axis in range(3)]
                for dz in (-1, 0, 1):
                    near = [wide_ref[found, item] for item in range(7)]
                    if dz:
                        near = [pltpu.roll(v, (-dz * A) % lanes, 1) for v in near]
                    r0 = at[0] - near[0] - shift_x
                    r1 = at[1] - near[1] - shift_y
                    r2 = at[2] - near[2] - float(dz * HZ)
                    square = r0 * r0 + r1 * r1 + r2 * r2
                    if dz == 0:
                        selfish = own & (step == 4)
                        square = jnp.where(selfish, 1.0, square)
                    inverse = lax.rsqrt(square)
                    inverse_square = inverse * inverse
                    distance = square * inverse
                    root_inverse = lax.rsqrt(polar * near[3])
                    t = 1.0 / (1.0 + (0.5 * BETA) * distance)
                    series = 0.17087277
                    for c in (-0.82215223, 1.48851587, -1.13520398, 0.27886807,
                              -0.18628806, 0.09678418, 0.37409196, 1.00002368, -1.26551223):
                        series = series * t + c
                    bell = jnp.exp((-BETA * BETA) * square)
                    screened = t * jnp.exp(series) * bell * inverse
                    gauss = (2.0 * BETA / ROOT_PI) * bell
                    first = (screened + gauss) * inverse_square
                    second = (3.0 * first + (2.0 * BETA * BETA) * gauss) * inverse_square
                    scaled = THOLE * square * distance * root_inverse
                    damping = jnp.exp(-scaled) * (inverse_square * inverse)
                    first = first - damping
                    second = second - 3.0 * (1.0 + scaled) * damping * inverse_square
                    if dz == 0:
                        first = jnp.where(selfish, 0.0, first)
                        second = jnp.where(selfish, 0.0, second)
                    projected = second * (r0 * near[4] + r1 * near[5] + r2 * near[6])
                    sums[0] = sums[0] + (projected * r0 - first * near[4])
                    sums[1] = sums[1] + (projected * r1 - first * near[5])
                    sums[2] = sums[2] + (projected * r2 - first * near[6])
                for axis in range(3):
                    sum_ref[axis] = sums[axis]
                return carry

            lax.fori_loop(0, 9, visit, 0)
            for axis in range(3):
                out_ref[axis, mine_l : mine_l + 1, :] = jnp.sum(
                    sum_ref[axis], axis=0, keepdims=True
                )


def total_field(far_ref, near_ref, moment, axis):
    field = near_ref[axis] + SELF_GAIN * moment

    def add(d, carry):
        return carry + far_ref[d, axis]

    return field + lax.fori_loop(0, far_ref.shape[0], add, jnp.zeros_like(moment), unroll=8)


def middle_kernel(cot_ref, gain_ref, moment_ref, near_ref, far_ref, send_ref, own_ref):
    cells_x = cot_ref.shape[1]
    devices = far_ref.shape[0]
    gain = gain_ref[...]
    parts = []
    for axis in range(3):
        field = total_field(far_ref, near_ref, moment_ref[axis], axis)
        cot = jnp.concatenate([cot_ref[axis, cx] for cx in range(cells_x)], axis=0)
        parts.append(gain * (cot + field))
    block = jnp.stack(parts, axis=0)
    own_ref[...] = block

    def put(d, carry):
        send_ref[d] = block
        return carry

    lax.fori_loop(0, devices, put, 0)


def last_kernel(cot_ref, gain_ref, moment_ref, near_ref, far_ref, out_ref):
    cells_x, cells_y = cot_ref.shape[1:3]
    gain = gain_ref[...]
    for axis in range(3):
        field = total_field(far_ref, near_ref, moment_ref[axis], axis)
        for cx in range(cells_x):
            rows = slice(cx * cells_y, (cx + 1) * cells_y)
            out_ref[axis, cx] = gain[rows] * (cot_ref[axis, cx] + field[rows])


def spaces(count, smem_first=False):
    found = [pl.BlockSpec(memory_space=pltpu.VMEM)] * count
    if smem_first:
        found[0] = pl.BlockSpec(memory_space=pltpu.SMEM)
    return found


def call(body, outs, ins, scratch=(), smem_first=False, flops=1000, limit=12):
    many = isinstance(outs, (list, tuple))
    return pl.pallas_call(
        body,
        out_shape=outs,
        in_specs=spaces(len(ins), smem_first),
        out_specs=spaces(len(outs)) if many else spaces(1)[0],
        scratch_shapes=list(scratch),
        compiler_params=pltpu.CompilerParams(vmem_limit_bytes=limit * MIB),
        cost_estimate=pl.CostEstimate(flops=flops, bytes_accessed=100000, transcendentals=0),
    )(*ins)


def green_values(grid_x, grid_y, grid_z, length_x, length_y, length_z):
    def part(grid, length):
        signed = jnp.where(2 * grid < length, grid, grid - length).astype(F32) / length
        angle = 2.0 * math.pi / length * grid.astype(F32)
        factor = 9.0 / ((2.0 + jnp.cos(angle)) * (2.0 + jnp.cos(angle)))
        return (signed * signed, factor)

    square_x, factor_x = part(grid_x, length_x)
    square_y, factor_y = part(grid_y, length_y)
    square_z, factor_z = part(grid_z, length_z)
    square = square_x + square_y + square_z
    anchor = (grid_x == 0) & (grid_y == 0) & (grid_z == 0)
    safe = jnp.where(anchor, 1.0, square)
    value = jnp.exp(-(math.pi / BETA) * (math.pi / BETA) * safe) / (math.pi * safe)
    value = value * factor_x * factor_y * factor_z / (length_x * length_y * length_z)
    return jnp.where(anchor | (grid_z >= length_z), 0.0, value)


def shards(cotangent, polarizability, site_offset, site_fraction, cell_count):
    _, cells_x, cells_y, lanes = cotangent.shape
    layers = cell_count.shape[2]
    devices_x = lax.axis_size("gx")
    devices_y = lax.axis_size("gy")
    devices = devices_x * devices_y
    columns = cells_x * cells_y
    total_x = devices_x * cells_x
    length_x = total_x * HX
    length_y = devices_y * cells_y * HY
    length_z = layers * HZ
    index_x = lax.axis_index("gx")
    index_y = lax.axis_index("gy")
    me = index_x * devices_y + index_y
    where = jnp.stack([index_x, index_y, me]).astype(jnp.int32)

    def exchange(value):
        return lax.all_to_all(value, AXES, split_axis=0, concat_axis=0, tiled=True)

    own_shape = jax.ShapeDtypeStruct((3, columns, lanes), F32)
    moment_shape = jax.ShapeDtypeStruct((devices, 3, columns, lanes), F32)
    send, gain, own = call(
        pack_kernel,
        [
            jax.ShapeDtypeStruct((devices, 7, columns, lanes), F32),
            jax.ShapeDtypeStruct((columns, lanes), F32),
            own_shape,
        ],
        [cotangent, polarizability, site_offset, site_fraction, cell_count],
        limit=58,
    )
    static = exchange(send)

    modes = me * MODES + jnp.arange(MODES, dtype=jnp.int32)
    green = green_values(
        jnp.arange(length_x, dtype=jnp.int32)[None, None, :],
        jnp.arange(length_y, dtype=jnp.int32)[None, :, None],
        modes[:, None, None],
        length_x,
        length_y,
        length_z,
    ).reshape(MODES * length_y, length_x)
    forward, inverse = x_tables(total_x, length_x)
    y_high, y_low = two_terms(cas_table(length_y))
    y_table = np.concatenate([y_high, y_low, y_high], axis=1)

    tall = length_y * MODES
    kept = devices if devices * columns <= 256 else 1
    far_scratch = [
        pltpu.VMEM((total_x // 4, tall, 4 * 2 * SPAN), F32),
        pltpu.VMEM((length_x // 128, tall, 128), F32),
        pltpu.VMEM((total_x // 2, tall + 32, 2 * 4 * SPAN), BF16),
    ]
    far_scratch = [
        pltpu.VMEM((kept, columns, 2 * SPAN, 2 * lanes), BF16),
        pltpu.VMEM((kept, columns, 2 * SPAN + 2 * MODES, lanes), F32),
    ] + far_scratch
    far_shape = (devices_x, devices_y, cells_x, cells_y, length_z)
    near_shape = (devices_x, devices_y, cells_x, cells_y)

    tables = [*(jnp.asarray(t) for t in (*forward, *inverse, y_table))]


    def far_first(where_ref, static_ref, *rest):
        far_kernel(far_shape, 3, where_ref, static_ref, static_ref, *rest)

    far_later = functools.partial(far_kernel, far_shape, 0)

    def near_first(where_ref, static_ref, *rest):
        near_kernel(near_shape, 3, where_ref, static_ref, static_ref, *rest)

    near_later = functools.partial(near_kernel, near_shape, 0)
    near_scratch = [
        pltpu.VMEM(((cells_x + 2) * (cells_y + 2) * 7 * A, lanes), F32),
        pltpu.VMEM(((cells_x + 2) * (cells_y + 2), 7, A, lanes), F32),
        pltpu.VMEM((3, A, lanes), F32),
    ]
    data = [where, static]
    for turn in range(ITERS):
        partial = call(
            far_later if turn else far_first,
            moment_shape,
            data + [green] + tables,
            far_scratch,
            smem_first=True,
            flops=10**9,
            limit=20 if kept > 1 else 60,
        )
        partial = exchange(partial)
        close = call(
            near_later if turn else near_first,
            own_shape,
            data,
            near_scratch,
            smem_first=True,
            flops=10**8,
        )
        ins = [cotangent, gain, own, close, partial]
        if turn < ITERS - 1:
            send, own = call(middle_kernel, [moment_shape, own_shape], ins)
            data = [where, static, exchange(send)]
        else:
            moment = call(last_kernel, jax.ShapeDtypeStruct(cotangent.shape, F32), ins)
    return moment


def solution(mesh):
    return jax.shard_map(
        shards,
        mesh=mesh,
        in_specs=(
            P(None, "gx", "gy", None),
            P("gx", "gy", None),
            P(None, "gx", "gy", None),
            P(None, "gx", "gy", None),
            P("gx", "gy", None),
        ),
        out_specs=P(None, "gx", "gy", None),
        check_vma=False,
    )
```

```python
import functools
import math

import jax
import jax.numpy as jnp
import ml_dtypes
import numpy as np
from jax import lax
from jax.experimental import pallas as pl
from jax.experimental.pallas import tpu as pltpu
from jax.sharding import PartitionSpec as P

A = 8
HX = 8
HY = 8
HZ = 16
ITERS = 2
BETA = 0.7
THOLE = 0.39
ROOT_PI = 1.7724538509055159
SELF_GAIN = 4.0 * BETA * BETA * BETA / (3.0 * ROOT_PI)
MODES = 8
SIXTH = 1.0 / 6.0
STATIC_UNROLL = 8
SPAN = 16
AXES = ("gx", "gy")
F32 = jnp.float32
BF16 = jnp.bfloat16
MIB = 1024 * 1024


def two_terms(table):
    high = table.astype(ml_dtypes.bfloat16)
    low = (table - high.astype(np.float64)).astype(ml_dtypes.bfloat16)
    return high, low


def cas_table(length):
    grid = np.arange(length, dtype=np.int64)
    angle = 2.0 * np.pi / length * (grid[:, None] * grid[None, :] % length)
    return np.cos(angle) + np.sin(angle)


def x_tables(cells, length):
    cas = cas_table(length)
    place = (np.arange(cells)[:, None] * HX + np.arange(SPAN)[None, :]) % length
    forward = np.broadcast_to(cas[place][:, None], (cells, 2, SPAN, length))
    forward = forward.reshape(cells // 4, 4 * 2 * SPAN, length)
    inverse = np.broadcast_to(cas[place][:, None], (cells, 4, SPAN, length))
    inverse = inverse.reshape(cells // 2, 2 * 4 * SPAN, length).transpose(0, 2, 1)
    return two_terms(forward), two_terms(inverse)


def split(value):
    high = value.astype(BF16)
    low = (value - high.astype(F32)).astype(BF16)
    return high, low


def dot(left, right):
    return jnp.dot(left, right, preferred_element_type=F32)


def dot_nt(left, right):
    return lax.dot_general(left, right, (((1,), (1,)), ((), ())), preferred_element_type=F32)


def spline(fraction):
    rest = 1.0 - fraction
    square = fraction * fraction
    cube = square * fraction
    values = (
        rest * rest * rest * SIXTH,
        (3.0 * cube - 6.0 * square + 4.0) * SIXTH,
        (-3.0 * cube + 3.0 * square + 3.0 * fraction + 1.0) * SIXTH,
        cube * SIXTH,
    )
    slopes = (
        -0.5 * rest * rest,
        0.5 * (3.0 * square - 4.0 * fraction),
        0.5 * (-3.0 * square + 2.0 * fraction + 1.0),
        0.5 * square,
    )
    return values, slopes


def basis(anchor, weights):
    lanes = anchor.shape[1]
    index = lax.broadcasted_iota(jnp.int32, (SPAN, lanes), 0) - anchor
    total = jnp.zeros((SPAN, lanes), F32)
    for order in range(4):
        total = jnp.where(index == order, weights[order], total)
    return total


def around(count, length):
    if length & (length - 1):
        return lax.rem(count, length)
    return count & (length - 1)


def turns(count, length):
    part = count.astype(F32) * (1.0 / length)
    half = math.pi * jnp.where(2 * count >= length, part - 1.0, part)
    square = half * half
    sine = 1.0
    for order in (10, 8, 6, 4, 2):
        sine = 1.0 - square * sine * (1.0 / (order * (order + 1)))
    sine = sine * half
    cosine = 1.0
    for order in (11, 9, 7, 5, 3, 1):
        cosine = 1.0 - square * cosine * (1.0 / (order * (order + 1)))
    return 1.0 - 2.0 * sine * sine, 2.0 * sine * cosine


def pack_kernel(cot_ref, polar_ref, offset_ref, fraction_ref, count_ref, send_ref, gain_ref, own_ref):
    cells_x, cells_y, lanes = polar_ref.shape
    devices = send_ref.shape[0]
    cells = lanes // A
    row = lax.broadcasted_iota(jnp.int32, (cells, lanes), 0)
    lane = lax.broadcasted_iota(jnp.int32, (cells, lanes), 1)
    widen = jnp.where(lane // A == row, 1.0, 0.0)
    slot = (lax.broadcasted_iota(jnp.int32, (cells_y, lanes), 1) % A).astype(F32)
    rows = [[] for _ in range(7)]
    gains = []
    for cx in range(cells_x):
        count = dot(count_ref[cx].astype(F32), widen)
        gain = jnp.where(slot < count, polar_ref[cx], 0.0)
        gains.append(gain)
        for axis in range(3):
            place = offset_ref[axis, cx].astype(F32) + 1.0 + fraction_ref[axis, cx]
            rows[axis].append(place)
            rows[3 + axis].append(gain * cot_ref[axis, cx])
        rows[6].append(polar_ref[cx])
    gain_ref[...] = jnp.concatenate(gains, axis=0)
    block = jnp.stack([jnp.concatenate(parts, axis=0) for parts in rows], axis=0)
    own_ref[...] = block[3:6]

    def put(d, carry):
        send_ref[d] = block
        return carry

    lax.fori_loop(0, devices, put, 0)


def far_kernel(
    shape,
    lead,
    where_ref,
    place_ref,
    moment_ref,
    green_ref,
    fx_high_ref,
    fx_low_ref,
    ix_high_ref,
    ix_low_ref,
    y_ref,
    out_ref,
    side_ref,
    form_ref,
    cell_ref,
    line_ref,
    wave_ref,
):
    edge = 2 * SPAN
    devices_x, devices_y, cells_x, cells_y, points_z = shape
    columns = cells_x * cells_y
    lanes = place_ref.shape[3]
    length_x = line_ref.shape[0] * line_ref.shape[2]
    tall = line_ref.shape[1]
    length_y = tall // MODES
    spill = 3 * MODES
    reach = (HY + 3) * MODES
    per_cell = HY * MODES
    turn_x = 4 // cells_x
    keep = form_ref.shape[0] > 1
    unroll = min(4, devices_y)
    layer = (lax.broadcasted_iota(jnp.int32, (1, lanes), 1) // A) * HZ
    mode = where_ref[2] * MODES + lax.broadcasted_iota(jnp.int32, (MODES, lanes), 0)
    plus, minus = [], []
    for order in range(4):
        cosine, sine = turns(lax.rem(mode * order, points_z), points_z)
        plus.append(cosine + sine)
        minus.append(cosine - sine)

    def statics(d):
        k = d if keep else 0
        place = [place_ref[d, axis] for axis in range(3)]
        whole = [jnp.floor(value) for value in place]
        parts = [spline(value - low) for value, low in zip(place, whole)]
        anchors = [low.astype(jnp.int32) - 1 for low in whole]
        for l in range(columns):
            row = slice(l, l + 1)
            anchor = [value[row] for value in anchors]
            weights = [[[v[row] for v in kind] for kind in part] for part in parts]
            slopes_x = basis(anchor[0], weights[0][1])
            values_x = basis(anchor[0], weights[0][0])
            high, low = split(jnp.concatenate([slopes_x, values_x], axis=1))
            side_ref[k, l] = jnp.concatenate([high, low], axis=0)
            form_ref[k, l, :edge] = jnp.concatenate(
                [basis(anchor[1], weights[1][0]), basis(anchor[1], weights[1][1])], axis=0
            )
            cosine, sine = turns(around(mode * (anchor[2] + layer), points_z), points_z)
            found = []
            for kind in weights[2]:
                up = kind[0] * plus[0]
                down = kind[0] * minus[0]
                for order in range(1, 4):
                    up = up + kind[order] * plus[order]
                    down = down + kind[order] * minus[order]
                found.append(cosine * up + sine * down)
            form_ref[k, l, edge:] = jnp.concatenate(found, axis=0)

    def spread_parts(d, l, slot):
        k = d if keep else 0
        first = form_ref[k, l, edge : edge + MODES] * moment_ref[d, lead, l : l + 1, :]
        second = form_ref[k, l, edge : edge + MODES] * moment_ref[d, lead + 1, l : l + 1, :]
        third = form_ref[k, l, edge + MODES :] * moment_ref[d, lead + 2, l : l + 1, :]
        tiles = []
        for y in range(HY + 3):
            value = form_ref[k, l, y : y + 1, :]
            slope = form_ref[k, l, SPAN + y : SPAN + y + 1, :]
            tile = jnp.concatenate([value * first, slope * second + value * third], axis=1)
            rest = tile - tile.astype(BF16).astype(F32)
            tiles.append(jnp.concatenate([tile, rest], axis=0).astype(BF16))
        pieces = []
        if slot:
            pieces.append(jnp.zeros((slot * 2 * SPAN, 2 * lanes), BF16))
        pieces.append(side_ref[k, l])
        if slot < 3:
            pieces.append(jnp.zeros(((3 - slot) * 2 * SPAN, 2 * lanes), BF16))
        return jnp.concatenate(tiles, axis=0), jnp.concatenate(pieces, axis=0)

    def prepare(d, carry):
        statics(d)
        return carry

    if keep:
        lax.fori_loop(0, devices_x * devices_y, prepare, 0, unroll=STATIC_UNROLL)

    def spread_row(pair, carry):
        def spread_device(gy, over):
            parts = [[] for _ in range(cells_y)]
            for odd in range(turn_x):
                d = (pair * turn_x + odd) * devices_y + gy
                if not keep:
                    statics(d)
                for l in range(columns):
                    left, right = spread_parts(d, l, odd * cells_x + l // cells_y)
                    parts[l % cells_y].append((left, right))
            for low in range(cells_y):
                start = pl.multiple_of((gy * cells_y + low) * per_cell, per_cell)
                left, right = (jnp.concatenate(part, axis=1) for part in zip(*parts[low]))
                got = dot_nt(left, right).reshape(HY + 3, 2, MODES, 8 * SPAN)
                got = (got[:, 0] + got[:, 1]).reshape(reach, 8 * SPAN)
                cell_ref[pair, pl.ds(start, spill), :] = got[:spill] + over
                cell_ref[pair, pl.ds(start + spill, per_cell - spill), :] = got[spill:per_cell]
                over = got[per_cell:]
            return over

        over = lax.fori_loop(
            0, devices_y, spread_device, jnp.zeros((spill, 8 * SPAN), F32), unroll=unroll
        )
        cell_ref[pair, :spill, :] = cell_ref[pair, :spill, :] + over
        return carry

    lax.fori_loop(0, devices_x // turn_x, spread_row, 0)

    total = jnp.zeros((tall, length_x), F32)
    for group in range(0, cell_ref.shape[0], 2):
        one_high, one_low = split(cell_ref[group])
        two_high, two_low = split(cell_ref[group + 1])
        one, two = fx_high_ref[group], fx_high_ref[group + 1]
        total = total + dot(
            jnp.concatenate([one_high, one_low], axis=1), jnp.concatenate([one, one], axis=0)
        )
        total = total + dot(
            jnp.concatenate([two_high, two_low], axis=1), jnp.concatenate([two, two], axis=0)
        )
        total = total + dot(
            jnp.concatenate([one_high, two_high], axis=1),
            jnp.concatenate([fx_low_ref[group], fx_low_ref[group + 1]], axis=0),
        )
    blocks = length_x // line_ref.shape[2]
    width = line_ref.shape[2]
    for block in range(blocks):
        line_ref[block] = total[:, block * width : (block + 1) * width]

    def along_y(value):
        high, low = split(value)
        return dot(y_ref[...], jnp.concatenate([high, high, low], axis=0))

    for block in range(blocks):
        found = []
        for number in range(MODES):
            got = along_y(line_ref[block, pl.ds(number, length_y, stride=MODES), :])
            found.append(
                got
                * green_ref[
                    number * length_y : (number + 1) * length_y,
                    block * width : (block + 1) * width,
                ]
            )
        for number in range(MODES):
            line_ref[block, pl.ds(number, length_y, stride=MODES), :] = along_y(found[number])
    high, low = split(jnp.concatenate([line_ref[block] for block in range(blocks)], axis=1))
    both = jnp.concatenate([high, low], axis=1)
    lane = lax.broadcasted_iota(jnp.int32, (tall, 4 * 4 * SPAN), 1)
    rest = lane // SPAN % 2 == 1
    for group in range(0, wave_ref.shape[0], 2):
        one = jnp.concatenate([ix_high_ref[group], ix_high_ref[group + 1]], axis=1)
        two = jnp.concatenate([ix_low_ref[group], ix_low_ref[group + 1]], axis=1)
        got = dot(both, jnp.concatenate([one, one], axis=0)) + dot(high, two)
        got = jnp.where(rest, got - got.astype(BF16).astype(F32), got).astype(BF16)
        for odd in range(2):
            part = got[:, odd * 8 * SPAN : (odd + 1) * 8 * SPAN]
            wave_ref[group + odd, :tall, :] = part
            wave_ref[group + odd, tall:, :] = part[: wave_ref.shape[1] - tall]

    window = -(-reach // 16) * 16

    def gather(d, l, slot, group, start):
        k = d if keep else 0
        found = side_ref[k, l]
        high, low = found[:SPAN], found[SPAN:]
        block = [high, high, low, low]
        zero = jnp.zeros((4 * SPAN, 2 * lanes), BF16)
        pieces = [zero] + block if slot else block + [zero]
        got = dot(wave_ref[group, pl.ds(start, window), :], jnp.concatenate(pieces, axis=0))
        sums = [jnp.zeros((MODES, lanes), F32) for _ in range(3)]
        for y in range(HY + 3):
            value = form_ref[k, l, y : y + 1, :]
            slope = form_ref[k, l, SPAN + y : SPAN + y + 1, :]
            sloped = got[y * MODES : (y + 1) * MODES, :lanes]
            plain = got[y * MODES : (y + 1) * MODES, lanes:]
            sums[0] = sums[0] + sloped * value
            sums[1] = sums[1] + plain * slope
            sums[2] = sums[2] + plain * value
        value = form_ref[k, l, edge : edge + MODES]
        slope = form_ref[k, l, edge + MODES :]
        return [
            -jnp.sum(sums[axis] * part, axis=0, keepdims=True)
            for axis, part in enumerate((value, value, slope))
        ]

    def gather_row(gx, carry):
        def gather_device(gy, inner):
            d = gx * devices_y + gy
            if not keep:
                statics(d)
            found = []
            for l in range(columns):
                across = l // cells_y
                start = pl.multiple_of((gy * cells_y + l % cells_y) * per_cell, per_cell)
                group = (gx * cells_x + across - across % 2) // 2
                found.append(gather(d, l, across % 2, group, start))
            for axis in range(3):
                out_ref[d, axis] = jnp.concatenate([part[axis] for part in found], axis=0)
            return inner

        lax.fori_loop(0, devices_y, gather_device, 0, unroll=unroll)
        return carry

    lax.fori_loop(0, devices_x, gather_row, 0)


def near_kernel(shape, lead, where_ref, static_ref, moment_ref, out_ref, raw_ref, wide_ref, sum_ref):
    devices_x, devices_y, cells_x, cells_y = shape
    lanes = static_ref.shape[3]
    rows_x, rows_y = cells_x + 2, cells_y + 2
    total_x, total_y = devices_x * cells_x, devices_y * cells_y
    lane = lax.broadcasted_iota(jnp.int32, (A, lanes), 1)
    sub = lax.broadcasted_iota(jnp.int32, (A, lanes), 0)
    own = lane % A == sub
    for a in range(rows_x):
        for b in range(rows_y):
            cell_x = lax.rem(where_ref[0] * cells_x + (a - 1 + total_x), total_x)
            cell_y = lax.rem(where_ref[1] * cells_y + (b - 1 + total_y), total_y)
            d = (cell_x // cells_x) * devices_y + cell_y // cells_y
            l = lax.rem(cell_x, cells_x) * cells_y + lax.rem(cell_y, cells_y)
            for item in range(7):
                if item < 4:
                    row = static_ref[d, item if item < 3 else 6, pl.ds(l, 1), :]
                else:
                    row = moment_ref[d, lead + item - 4, pl.ds(l, 1), :]
                first = ((a * rows_y + b) * 7 + item) * A
                raw_ref[first : first + A, :] = jnp.where(own, row, 0.0)
    group = lax.broadcasted_iota(jnp.int32, (lanes, lanes), 0) // A
    other = lax.broadcasted_iota(jnp.int32, (lanes, lanes), 1) // A
    ones = jnp.where(group == other, 1.0, 0.0).astype(BF16)
    raw = raw_ref[...]
    high = raw.astype(BF16)
    raw = raw - high.astype(F32)
    middle = raw.astype(BF16)
    low = (raw - middle.astype(F32)).astype(BF16)
    wide = dot(low, ones) + dot(middle, ones) + dot(high, ones)
    wide_ref[...] = wide.reshape(wide_ref.shape)

    for across in range(cells_x):
        for along in range(cells_y):
            mine = (across + 1) * rows_y + along + 1
            mine_d = where_ref[0] * devices_y + where_ref[1]
            mine_l = across * cells_y + along
            at = [static_ref[mine_d, axis, mine_l : mine_l + 1, :] for axis in range(3)]
            polar = static_ref[mine_d, 6, mine_l : mine_l + 1, :]
            sum_ref[...] = jnp.zeros_like(sum_ref)

            def visit(step, carry, across=across, along=along, at=at, polar=polar):
                dx = step // 3 - 1
                dy = lax.rem(step, 3) - 1
                found = (across + 1 + dx) * rows_y + along + 1 + dy
                shift_x = dx.astype(F32) * HX
                shift_y = dy.astype(F32) * HY
                sums = [sum_ref[axis] for axis in range(3)]
                for dz in (-1, 0, 1):
                    near = [wide_ref[found, item] for item in range(7)]
                    if dz:
                        near = [pltpu.roll(v, (-dz * A) % lanes, 1) for v in near]
                    r0 = at[0] - near[0] - shift_x
                    r1 = at[1] - near[1] - shift_y
                    r2 = at[2] - near[2] - float(dz * HZ)
                    square = r0 * r0 + r1 * r1 + r2 * r2
                    if dz == 0:
                        selfish = own & (step == 4)
                        square = jnp.where(selfish, 1.0, square)
                    inverse = lax.rsqrt(square)
                    inverse_square = inverse * inverse
                    distance = square * inverse
                    root_inverse = lax.rsqrt(polar * near[3])
                    t = 1.0 / (1.0 + (0.5 * BETA) * distance)
                    series = 0.17087277
                    for c in (-0.82215223, 1.48851587, -1.13520398, 0.27886807,
                              -0.18628806, 0.09678418, 0.37409196, 1.00002368, -1.26551223):
                        series = series * t + c
                    bell = jnp.exp((-BETA * BETA) * square)
                    screened = t * jnp.exp(series) * bell * inverse
                    gauss = (2.0 * BETA / ROOT_PI) * bell
                    first = (screened + gauss) * inverse_square
                    second = (3.0 * first + (2.0 * BETA * BETA) * gauss) * inverse_square
                    scaled = THOLE * square * distance * root_inverse
                    damping = jnp.exp(-scaled) * (inverse_square * inverse)
                    first = first - damping
                    second = second - 3.0 * (1.0 + scaled) * damping * inverse_square
                    if dz == 0:
                        first = jnp.where(selfish, 0.0, first)
                        second = jnp.where(selfish, 0.0, second)
                    projected = second * (r0 * near[4] + r1 * near[5] + r2 * near[6])
                    sums[0] = sums[0] + (projected * r0 - first * near[4])
                    sums[1] = sums[1] + (projected * r1 - first * near[5])
                    sums[2] = sums[2] + (projected * r2 - first * near[6])
                for axis in range(3):
                    sum_ref[axis] = sums[axis]
                return carry

            lax.fori_loop(0, 9, visit, 0)
            for axis in range(3):
                out_ref[axis, mine_l : mine_l + 1, :] = jnp.sum(
                    sum_ref[axis], axis=0, keepdims=True
                )


def total_field(far_ref, near_ref, moment, axis):
    field = near_ref[axis] + SELF_GAIN * moment

    def add(d, carry):
        return carry + far_ref[d, axis]

    return field + lax.fori_loop(0, far_ref.shape[0], add, jnp.zeros_like(moment), unroll=8)


def middle_kernel(cot_ref, gain_ref, moment_ref, near_ref, far_ref, send_ref, own_ref):
    cells_x = cot_ref.shape[1]
    devices = far_ref.shape[0]
    gain = gain_ref[...]
    parts = []
    for axis in range(3):
        field = total_field(far_ref, near_ref, moment_ref[axis], axis)
        cot = jnp.concatenate([cot_ref[axis, cx] for cx in range(cells_x)], axis=0)
        parts.append(gain * (cot + field))
    block = jnp.stack(parts, axis=0)
    own_ref[...] = block

    def put(d, carry):
        send_ref[d] = block
        return carry

    lax.fori_loop(0, devices, put, 0)


def last_kernel(cot_ref, gain_ref, moment_ref, near_ref, far_ref, out_ref):
    cells_x, cells_y = cot_ref.shape[1:3]
    gain = gain_ref[...]
    for axis in range(3):
        field = total_field(far_ref, near_ref, moment_ref[axis], axis)
        for cx in range(cells_x):
            rows = slice(cx * cells_y, (cx + 1) * cells_y)
            out_ref[axis, cx] = gain[rows] * (cot_ref[axis, cx] + field[rows])


def spaces(count, smem_first=False):
    found = [pl.BlockSpec(memory_space=pltpu.VMEM)] * count
    if smem_first:
        found[0] = pl.BlockSpec(memory_space=pltpu.SMEM)
    return found


def call(body, outs, ins, scratch=(), smem_first=False, flops=1000, limit=12):
    many = isinstance(outs, (list, tuple))
    return pl.pallas_call(
        body,
        out_shape=outs,
        in_specs=spaces(len(ins), smem_first),
        out_specs=spaces(len(outs)) if many else spaces(1)[0],
        scratch_shapes=list(scratch),
        compiler_params=pltpu.CompilerParams(vmem_limit_bytes=limit * MIB),
        cost_estimate=pl.CostEstimate(flops=flops, bytes_accessed=100000, transcendentals=0),
    )(*ins)


def green_values(grid_x, grid_y, grid_z, length_x, length_y, length_z):
    def part(grid, length):
        signed = jnp.where(2 * grid < length, grid, grid - length).astype(F32) / length
        angle = 2.0 * math.pi / length * grid.astype(F32)
        factor = 9.0 / ((2.0 + jnp.cos(angle)) * (2.0 + jnp.cos(angle)))
        return (signed * signed, factor)

    square_x, factor_x = part(grid_x, length_x)
    square_y, factor_y = part(grid_y, length_y)
    square_z, factor_z = part(grid_z, length_z)
    square = square_x + square_y + square_z
    anchor = (grid_x == 0) & (grid_y == 0) & (grid_z == 0)
    safe = jnp.where(anchor, 1.0, square)
    value = jnp.exp(-(math.pi / BETA) * (math.pi / BETA) * safe) / (math.pi * safe)
    value = value * factor_x * factor_y * factor_z / (length_x * length_y * length_z)
    return jnp.where(anchor | (grid_z >= length_z), 0.0, value)


def shards(cotangent, polarizability, site_offset, site_fraction, cell_count):
    _, cells_x, cells_y, lanes = cotangent.shape
    layers = cell_count.shape[2]
    devices_x = lax.axis_size("gx")
    devices_y = lax.axis_size("gy")
    devices = devices_x * devices_y
    columns = cells_x * cells_y
    total_x = devices_x * cells_x
    length_x = total_x * HX
    length_y = devices_y * cells_y * HY
    length_z = layers * HZ
    index_x = lax.axis_index("gx")
    index_y = lax.axis_index("gy")
    me = index_x * devices_y + index_y
    where = jnp.stack([index_x, index_y, me]).astype(jnp.int32)

    def exchange(value):
        return lax.all_to_all(value, AXES, split_axis=0, concat_axis=0, tiled=True)

    own_shape = jax.ShapeDtypeStruct((3, columns, lanes), F32)
    moment_shape = jax.ShapeDtypeStruct((devices, 3, columns, lanes), F32)
    send, gain, own = call(
        pack_kernel,
        [
            jax.ShapeDtypeStruct((devices, 7, columns, lanes), F32),
            jax.ShapeDtypeStruct((columns, lanes), F32),
            own_shape,
        ],
        [cotangent, polarizability, site_offset, site_fraction, cell_count],
        limit=58,
    )
    static = exchange(send)

    modes = me * MODES + jnp.arange(MODES, dtype=jnp.int32)
    green = green_values(
        jnp.arange(length_x, dtype=jnp.int32)[None, None, :],
        jnp.arange(length_y, dtype=jnp.int32)[None, :, None],
        modes[:, None, None],
        length_x,
        length_y,
        length_z,
    ).reshape(MODES * length_y, length_x)
    forward, inverse = x_tables(total_x, length_x)
    y_high, y_low = two_terms(cas_table(length_y))
    y_table = np.concatenate([y_high, y_low, y_high], axis=1)

    tall = length_y * MODES
    kept = devices if devices * columns <= 256 else 1
    far_scratch = [
        pltpu.VMEM((total_x // 4, tall, 4 * 2 * SPAN), F32),
        pltpu.VMEM((length_x // 128, tall, 128), F32),
        pltpu.VMEM((total_x // 2, tall + 32, 2 * 4 * SPAN), BF16),
    ]
    far_scratch = [
        pltpu.VMEM((kept, columns, 2 * SPAN, 2 * lanes), BF16),
        pltpu.VMEM((kept, columns, 2 * SPAN + 2 * MODES, lanes), F32),
    ] + far_scratch
    far_shape = (devices_x, devices_y, cells_x, cells_y, length_z)
    near_shape = (devices_x, devices_y, cells_x, cells_y)

    tables = [*(jnp.asarray(t) for t in (*forward, *inverse, y_table))]


    def far_first(where_ref, static_ref, *rest):
        far_kernel(far_shape, 3, where_ref, static_ref, static_ref, *rest)

    far_later = functools.partial(far_kernel, far_shape, 0)

    def near_first(where_ref, static_ref, *rest):
        near_kernel(near_shape, 3, where_ref, static_ref, static_ref, *rest)

    near_later = functools.partial(near_kernel, near_shape, 0)
    near_scratch = [
        pltpu.VMEM(((cells_x + 2) * (cells_y + 2) * 7 * A, lanes), F32),
        pltpu.VMEM(((cells_x + 2) * (cells_y + 2), 7, A, lanes), F32),
        pltpu.VMEM((3, A, lanes), F32),
    ]
    data = [where, static]
    for turn in range(ITERS):
        partial = call(
            far_later if turn else far_first,
            moment_shape,
            data + [green] + tables,
            far_scratch,
            smem_first=True,
            flops=10**9,
            limit=20 if kept > 1 else 60,
        )
        partial = exchange(partial)
        close = call(
            near_later if turn else near_first,
            own_shape,
            data,
            near_scratch,
            smem_first=True,
            flops=10**8,
        )
        ins = [cotangent, gain, own, close, partial]
        if turn < ITERS - 1:
            send, own = call(middle_kernel, [moment_shape, own_shape], ins)
            data = [where, static, exchange(send)]
        else:
            moment = call(last_kernel, jax.ShapeDtypeStruct(cotangent.shape, F32), ins)
    return moment


def solution(mesh):
    return jax.shard_map(
        shards,
        mesh=mesh,
        in_specs=(
            P(None, "gx", "gy", None),
            P("gx", "gy", None),
            P(None, "gx", "gy", None),
            P(None, "gx", "gy", None),
            P("gx", "gy", None),
        ),
        out_specs=P(None, "gx", "gy", None),
        check_vma=False,
    )
```
